128 devices in a mesh: seq: 64 (over z, y, x_hi, core), head: 2 (over x_lo).
Axes of the slice: x: 4 (x_hi: 2, x_lo: 2; x = x_hi * 2 + x_lo), y: 4, z: 4, core: 2. Of those that a mesh axis runs over, the one named last changes fastest.
Arguments:
- queries: bfloat16 [32768, 5120], P(('seq', 'head')), may hold values from -8 to 8
- keys: bfloat16 [32768, 1024], P(('seq', 'head')), may hold values from -8 to 8
- values: bfloat16 [32768, 1024], P(('seq', 'head')), may hold values from -6 to 6
- output_gradient: bfloat16 [32768, 5120], P(('seq', 'head')), may hold values from -6 to 6
- document_lengths: int32 [64, 16], replicated, may hold values from 1 to 377, as said below
Outputs:
- attn_out: bfloat16 [32768, 5120], P(('seq', 'head'))
- query_grad: bfloat16 [32768, 5120], P(('seq', 'head'))
- key_grad: bfloat16 [32768, 1024], P(('seq', 'head'))
- value_grad: bfloat16 [32768, 1024], P(('seq', 'head'))
The draws below stay inside these ranges and needn't reach their ends.
Inputs may be any that keep to these rules, and one draw needn't show every extreme that they name: `document_lengths`: every entry of a row is 1 or more; a row sums to 512; its last 8 entries sum to 128, so no document crosses the start of a block's last 128 tokens.
All inputs are finite; a program needn't handle non-finite values.
Results may differ from the reference program's by a relative error of at most 0.012.
The reference program's roundings to bfloat16 on the way (of `probs_bf` and `dscores`) count: a program that leaves them out, or rounds other values in their place, can miss the bound.
Values may be sent and summed in bfloat16 or wider, within the bound.
A program may use at most 128 MiB of HBM per device.

```python
import math
import jax
import jax.numpy as jnp
from jax import lax

QUERY_HEAD_COUNT = 40
KEY_VALUE_HEADS = 8
HEAD_SIZE = 128
HALF_DOCS = 8
BLOCK_TOKENS = 512
TAIL = 128
DOCUMENT_BLOCKS = 64
TOKEN_TOTAL = 32768


def draw_queries(key, part):
    key = jax.random.fold_in(key, 21)
    base_offset = jnp.clip(jax.random.normal(key, (TOKEN_TOTAL, QUERY_HEAD_COUNT * HEAD_SIZE), jnp.float32), -6.0, 6.0)
    return base_offset.astype(jnp.bfloat16)


def draw_keys(key, part):
    key = jax.random.fold_in(key, 33)
    base_offset = jnp.clip(jax.random.normal(key, (TOKEN_TOTAL, KEY_VALUE_HEADS * HEAD_SIZE), jnp.float32), -6.0, 6.0)
    return base_offset.astype(jnp.bfloat16)


def compose(key, total):
    cuts = jnp.sort(jax.random.permutation(key, total - 1)[:HALF_DOCS - 1] + 1).astype(jnp.int32)
    edges = jnp.concatenate([jnp.zeros((1,), jnp.int32), cuts, jnp.full((1,), total, jnp.int32)])
    return (edges[1:] - edges[:-1]).astype(jnp.int32)


def long_first(total):
    return jnp.concatenate([jnp.full((1,), total - HALF_DOCS + 1, jnp.int32), jnp.ones((HALF_DOCS - 1,), jnp.int32)])


def draw_document_lengths(key, part):
    key = jax.random.fold_in(key, 11)
    front = BLOCK_TOKENS - TAIL
    heavy = jax.random.randint(jax.random.fold_in(key, 1), (DOCUMENT_BLOCKS, 2), 0, 2).astype(jnp.int32)
    shard = jnp.arange(DOCUMENT_BLOCKS, dtype=jnp.int32)[:, None]
    heavy = jnp.where(shard == 0, 1, jnp.where(shard == DOCUMENT_BLOCKS // 2, 0, heavy))
    light_front = jax.vmap(lambda k: compose(k, front))(jax.random.split(jax.random.fold_in(key, 2), DOCUMENT_BLOCKS))
    light_tail = jax.vmap(lambda k: compose(k, TAIL))(jax.random.split(jax.random.fold_in(key, 3), DOCUMENT_BLOCKS))
    front_part = jnp.where(heavy[:, 0:1] == 1, long_first(front)[None, :], light_front)
    tail_part = jnp.where(heavy[:, 1:2] == 1, long_first(TAIL)[None, :], light_tail)
    return jnp.concatenate([front_part, tail_part], axis=1).astype(jnp.int32)


def shard_levels(rng, shape, cuts, least, top_value):
    level, own = 1.0, jax.random.fold_in(rng, 6)
    for position, blocks in cuts:
        heights = jnp.exp(jax.random.uniform(jax.random.fold_in(own, position), (blocks,), jnp.float32, least / len(cuts), top_value / len(cuts)))
        level = level * jnp.repeat(heights, shape[position] // blocks).reshape([-1 if axis == position else 1 for axis in range(len(shape))])
    return level


def noise(own_key, shape, scale, limit, pieces=(), held_as=jnp.bfloat16):
    level = shard_levels(own_key, shape, pieces, -0.22, 0.18) if pieces else 1.0
    array = jax.random.normal(own_key, shape, jnp.float32) * scale * level
    return jnp.minimum(jnp.maximum(array, -limit), limit).astype(held_as)


def setup_inputs(seed: int = 0) -> dict:
    streams_of = jax.random.split(jax.random.key(seed), 6)
    return {
        "queries": draw_queries(jax.random.fold_in(streams_of[5], 71), 0),
        "keys": draw_keys(jax.random.fold_in(streams_of[5], 71), 0),
        "values": noise(streams_of[2], (TOKEN_TOTAL, KEY_VALUE_HEADS * HEAD_SIZE), 1.0, 6.0, ((0, 128),)),
        "output_gradient": noise(streams_of[3], (TOKEN_TOTAL, QUERY_HEAD_COUNT * HEAD_SIZE), 1.0, 6.0, ((0, 128),)),
        "document_lengths": draw_document_lengths(jax.random.fold_in(streams_of[5], 71), 0),
    }


NEG = -1e+30

def doc_ids(lengths_row, count):
    starts = jnp.cumsum(lengths_row) - lengths_row
    place = jnp.arange(count, dtype=jnp.int32)
    return lax.optimization_barrier(jnp.sum((place[:, None] >= starts[None, :]).astype(jnp.int32), axis=1)) - 1

def visibility(query_doc, query_pos, key_doc, key_pos):
    return (query_doc[:, None] == key_doc[None, :]) & (key_pos[None, :] <= query_pos[:, None])

def head_pass(query_head, key_head, value_head, grad_head, visible, scale):
    scores = jnp.dot(query_head.astype(jnp.float32), key_head.astype(jnp.float32).T) * scale
    scores = jnp.where(visible, scores, NEG)
    top = lax.optimization_barrier(jnp.max(scores, axis=1, keepdims=True))
    lse = top + jnp.log(lax.optimization_barrier(jnp.sum(jnp.exp(scores - top), axis=1, keepdims=True)))
    probs = jnp.where(visible, jnp.exp(scores - lse), 0.0)
    probs_bf = probs.astype(jnp.bfloat16)
    attention_output = jnp.dot(probs_bf, value_head, preferred_element_type=jnp.float32).astype(jnp.bfloat16)
    delta = lax.optimization_barrier(jnp.sum(grad_head.astype(jnp.float32) * attention_output.astype(jnp.float32), axis=1, keepdims=True))
    dprobs = jnp.dot(grad_head, value_head.T, preferred_element_type=jnp.float32)
    dscores = (probs * (dprobs - delta)).astype(jnp.bfloat16)
    query_grad = (jnp.dot(dscores, key_head, preferred_element_type=jnp.float32) * scale).astype(jnp.bfloat16)
    key_part = jnp.dot(dscores.T, query_head, preferred_element_type=jnp.float32) * scale
    value_part = jnp.dot(probs_bf.T, grad_head, preferred_element_type=jnp.float32)
    return (attention_output, query_grad, key_part, value_part)

def reference(queries, keys, values, output_gradient, document_lengths):
    group_ratio = QUERY_HEAD_COUNT // KEY_VALUE_HEADS
    scale = 1.0 / math.sqrt(HEAD_SIZE)

    def one_block(items):
        qrows, key_row_block, value_row_block, grows, lengths_row = items
        ids = doc_ids(lengths_row, BLOCK_TOKENS)
        place = jnp.arange(BLOCK_TOKENS, dtype=jnp.int32)
        visible = visibility(ids, place, ids, place)
        qheads = qrows.reshape(BLOCK_TOKENS, QUERY_HEAD_COUNT, HEAD_SIZE).transpose(1, 0, 2)
        gheads = grows.reshape(BLOCK_TOKENS, QUERY_HEAD_COUNT, HEAD_SIZE).transpose(1, 0, 2)
        key_head_rows = key_row_block.reshape(BLOCK_TOKENS, KEY_VALUE_HEADS, HEAD_SIZE).transpose(1, 0, 2)
        value_head_rows = value_row_block.reshape(BLOCK_TOKENS, KEY_VALUE_HEADS, HEAD_SIZE).transpose(1, 0, 2)
        group = (jnp.arange(QUERY_HEAD_COUNT, dtype=jnp.int32) // group_ratio).astype(jnp.int32)

        def per_head(parts):
            qh, gh, index = parts
            return head_pass(qh, key_head_rows[index], value_head_rows[index], gh, visible, scale)
        attention_output, query_gradient, key_portion, value_portion = lax.map(per_head, (qheads, gheads, group))
        key_gradient = lax.optimization_barrier(jnp.sum(key_portion.reshape(KEY_VALUE_HEADS, group_ratio, BLOCK_TOKENS, HEAD_SIZE), axis=1)).astype(jnp.bfloat16)
        value_gradient = lax.optimization_barrier(jnp.sum(value_portion.reshape(KEY_VALUE_HEADS, group_ratio, BLOCK_TOKENS, HEAD_SIZE), axis=1)).astype(jnp.bfloat16)
        attention_output = attention_output.transpose(1, 0, 2).reshape(BLOCK_TOKENS, QUERY_HEAD_COUNT * HEAD_SIZE)
        query_gradient = query_gradient.transpose(1, 0, 2).reshape(BLOCK_TOKENS, QUERY_HEAD_COUNT * HEAD_SIZE)
        key_gradient = key_gradient.transpose(1, 0, 2).reshape(BLOCK_TOKENS, KEY_VALUE_HEADS * HEAD_SIZE)
        value_gradient = value_gradient.transpose(1, 0, 2).reshape(BLOCK_TOKENS, KEY_VALUE_HEADS * HEAD_SIZE)
        return (attention_output, query_gradient, key_gradient, value_gradient)
    block_list = (queries.reshape(DOCUMENT_BLOCKS, BLOCK_TOKENS, QUERY_HEAD_COUNT * HEAD_SIZE), keys.reshape(DOCUMENT_BLOCKS, BLOCK_TOKENS, KEY_VALUE_HEADS * HEAD_SIZE), values.reshape(DOCUMENT_BLOCKS, BLOCK_TOKENS, KEY_VALUE_HEADS * HEAD_SIZE), output_gradient.reshape(DOCUMENT_BLOCKS, BLOCK_TOKENS, QUERY_HEAD_COUNT * HEAD_SIZE), document_lengths)
    attention_output, query_gradient, key_gradient, value_gradient = lax.map(one_block, block_list)
    return (attention_output.reshape(TOKEN_TOTAL, QUERY_HEAD_COUNT * HEAD_SIZE), query_gradient.reshape(TOKEN_TOTAL, QUERY_HEAD_COUNT * HEAD_SIZE), key_gradient.reshape(TOKEN_TOTAL, KEY_VALUE_HEADS * HEAD_SIZE), value_gradient.reshape(TOKEN_TOTAL, KEY_VALUE_HEADS * HEAD_SIZE))
```

```python
import functools
import math

import jax
import jax.numpy as jnp
from jax import lax
from jax.experimental import pallas as pl
from jax.experimental.pallas import tpu as pltpu
from jax.sharding import PartitionSpec as P

QUERY_HEADS = 40
GROUPS = 8
RATIO = QUERY_HEADS // GROUPS
WIDTH = 128
WIDE = RATIO * WIDTH
ROWS = 256
HALF = 128
DOCS = 16
NEG = -1e30
SCALE = 1.0 / math.sqrt(WIDTH)
TO_EXP2 = SCALE * math.log2(math.e)
MESH = pl.DeviceIdType.MESH
F32 = jnp.float32
BF16 = jnp.bfloat16


def dot_nt(a, b):
    return lax.dot_general(a, b, (((1,), (1,)), ((), ())), preferred_element_type=F32)


def dot_nn(a, b):
    return jnp.dot(a, b, preferred_element_type=F32)


def stacked(ref, row, group):
    return jnp.concatenate(
        [
            ref[pl.ds(row, HALF), pl.ds(pl.multiple_of(group * WIDE + h * WIDTH, WIDTH), WIDTH)]
            for h in range(RATIO)
        ],
        axis=0,
    )


def columns(group):
    return pl.ds(pl.multiple_of(group * WIDTH, WIDTH), WIDTH)


def probabilities(keys, queries, bias):
    logits = dot_nt(keys, queries) * TO_EXP2 + jnp.concatenate([bias] * RATIO, axis=1)
    weights = jnp.exp2(logits - jnp.max(logits, axis=0, keepdims=True))
    return weights * (1.0 / jnp.sum(weights, axis=0, keepdims=True))


def score_gradient(probs, values, grads):
    dprobs = dot_nt(values, grads)
    delta = jnp.sum(probs * dprobs, axis=0, keepdims=True)
    return (probs * (dprobs - delta)).astype(BF16)


def put_heads(ref, row, group, transposed):
    for h in range(RATIO):
        block = transposed[:, h * WIDTH : (h + 1) * WIDTH].T
        where = pl.ds(pl.multiple_of(group * WIDE + h * WIDTH, WIDTH), WIDTH)
        ref[pl.ds(row, HALF), where] = block.astype(BF16)


def mask_bias(lengths, block, first_query, first_key, keys):
    query = first_query + lax.broadcasted_iota(jnp.int32, (1, HALF), 1)
    start = jnp.int32(0)
    doc_start = jnp.zeros((1, HALF), jnp.int32)
    for d in range(DOCS):
        doc_start = jnp.where(query >= start, start, doc_start)
        start = start + lengths[block, d]
    key = first_key + lax.broadcasted_iota(jnp.int32, (keys, HALF), 0)
    return jnp.where((key >= doc_start) & (key <= query), 0.0, NEG).astype(F32)


def kernel(
    lengths_hbm, q_hbm, k_hbm, v_hbm, g_hbm,
    o_out, dq_out, dk_out, dv_out,
    q_own, k_own, v_own, g_own,
    k_far, v_far, dk_send, dv_send, dk_far, dv_far, dk_sum, dv_sum,
    bias_a, bias_b, lengths, lengths_sem, load_sem, send_sem, recv_sem,
):
    seq = lax.axis_index("seq")
    head = lax.axis_index("head")
    partner = (seq, 1 - head)
    barrier = pltpu.get_barrier_semaphore()
    pl.semaphore_signal(barrier, inc=1, device_id=partner, device_id_type=MESH)

    lengths_copy = pltpu.make_async_copy(lengths_hbm, lengths, lengths_sem)
    lengths_copy.start()

    def loads(g):
        wide = pl.ds(pl.multiple_of(g * WIDE, WIDTH), WIDE)
        return [
            pltpu.make_async_copy(src.at[:, where], dst.at[:, where], load_sem.at[i, g])
            for i, (src, dst, where) in enumerate(
                (
                    (k_hbm, k_own, columns(g)),
                    (q_hbm, q_own, wide),
                    (g_hbm, g_own, wide),
                    (v_hbm, v_own, columns(g)),
                )
            )
        ]

    def far(i, g):
        src, dst = (
            (k_hbm.at[:, columns(g)], k_far.at[g]),
            (v_hbm.at[:, columns(g)], v_far.at[g]),
            (dv_send.at[g], dv_far.at[g]),
            (dk_send.at[g], dk_far.at[g]),
        )[i]
        return pltpu.make_async_remote_copy(
            src_ref=src,
            dst_ref=dst,
            send_sem=send_sem.at[i, g],
            recv_sem=recv_sem.at[i, g],
            device_id=partner,
            device_id_type=MESH,
        )

    def start_loads(g, _):
        for copy in loads(g):
            copy.start()
        return 0

    lax.fori_loop(0, GROUPS, start_loads, 0)
    lengths_copy.wait()
    pl.semaphore_wait(barrier, 1)

    @pl.when(head == 0)
    def _():
        def send(g, _):
            far(0, g).start()
            far(1, g).start()
            return 0

        lax.fori_loop(0, GROUPS, send, 0)
        bias_a[0:ROWS] = mask_bias(lengths, seq, HALF, 0, ROWS)
        bias_b[...] = mask_bias(lengths, seq, 0, 0, HALF)

        def local(g, _):
            for copy in loads(g):
                copy.wait()
            for row, keys, bias in ((HALF, ROWS, bias_a), (0, HALF, bias_b)):
                kk = k_own[0:keys, columns(g)]
                vv = v_own[0:keys, columns(g)]
                qq = stacked(q_own, row, g)
                gg = stacked(g_own, row, g)
                probs = probabilities(kk, qq, bias[0:keys])
                rounded = probs.astype(BF16)
                dscores = score_gradient(probs, vv, gg)
                dv = dot_nn(rounded, gg)
                dk = dot_nn(dscores, qq)
                if row:
                    dv_sum[g] = dv
                    dk_sum[g] = dk
                else:
                    dv_sum[g, 0:HALF] += dv
                    dk_sum[g, 0:HALF] += dk
                put_heads(o_out, row, g, dot_nn(vv.T, rounded))
                put_heads(dq_out, row, g, dot_nn(kk.T, dscores) * SCALE)
            return 0

        lax.fori_loop(0, GROUPS, local, 0)

        def finish(g, _):
            far(2, g).wait_recv()
            dv_out[:, columns(g)] = (dv_sum[g] + dv_far[g].astype(F32)).astype(BF16)
            far(3, g).wait_recv()
            dk_out[:, columns(g)] = (dk_sum[g] * SCALE + dk_far[g].astype(F32)).astype(BF16)
            return 0

        lax.fori_loop(0, GROUPS, finish, 0)

        def drain(g, _):
            far(0, g).wait_send()
            far(1, g).wait_send()
            return 0

        lax.fori_loop(0, GROUPS, drain, 0)

    @pl.when(head == 1)
    def _():
        bias_a[...] = mask_bias(lengths, seq, ROWS, 0, ROWS + HALF)
        bias_b[...] = mask_bias(lengths, seq, ROWS + HALF, ROWS + HALF, HALF)

        def work(g, _):
            for copy in loads(g):
                copy.wait()
            kk = k_own[HALF:ROWS, columns(g)]
            vv = v_own[HALF:ROWS, columns(g)]
            qq = stacked(q_own, HALF, g)
            gg = stacked(g_own, HALF, g)
            probs = probabilities(kk, qq, bias_b[...])
            rounded = probs.astype(BF16)
            dscores = score_gradient(probs, vv, gg)
            dv_out[HALF:ROWS, columns(g)] = dot_nn(rounded, gg).astype(BF16)
            dk_out[HALF:ROWS, columns(g)] = (dot_nn(dscores, qq) * SCALE).astype(BF16)
            put_heads(o_out, HALF, g, dot_nn(vv.T, rounded))
            put_heads(dq_out, HALF, g, dot_nn(kk.T, dscores) * SCALE)

            far(0, g).wait_recv()
            kk = jnp.concatenate([k_far[g], k_own[0:HALF, columns(g)]], axis=0)
            qq = stacked(q_own, 0, g)
            gg = stacked(g_own, 0, g)
            probs = probabilities(kk, qq, bias_a[...])
            rounded = probs.astype(BF16)
            dv = dot_nn(rounded, gg).astype(BF16)
            dv_send[g] = dv[0:ROWS]
            far(2, g).start()
            dv_out[0:HALF, columns(g)] = dv[ROWS:]
            far(1, g).wait_recv()
            vv = jnp.concatenate([v_far[g], v_own[0:HALF, columns(g)]], axis=0)
            dscores = score_gradient(probs, vv, gg)
            dk = (dot_nn(dscores, qq) * SCALE).astype(BF16)
            dk_send[g] = dk[0:ROWS]
            far(3, g).start()
            dk_out[0:HALF, columns(g)] = dk[ROWS:]
            put_heads(o_out, 0, g, dot_nn(vv.T, rounded))
            put_heads(dq_out, 0, g, dot_nn(kk.T, dscores) * SCALE)
            return 0

        lax.fori_loop(0, GROUPS, work, 0)

        def drain(g, _):
            far(2, g).wait_send()
            far(3, g).wait_send()
            return 0

        lax.fori_loop(0, GROUPS, drain, 0)


def body(queries, keys, values, output_gradient, document_lengths):
    hbm = pl.BlockSpec(memory_space=pl.ANY)
    block = pltpu.VMEM((GROUPS, ROWS, WIDTH), BF16)
    total = pltpu.VMEM((GROUPS, ROWS, WIDTH), F32)
    return pl.pallas_call(
        kernel,
        out_shape=[pltpu.VMEM(x.shape, BF16) for x in (queries, queries, keys, values)],
        in_specs=[hbm] * 5,
        scratch_shapes=[
            pltpu.VMEM(queries.shape, BF16),
            pltpu.VMEM(keys.shape, BF16),
            pltpu.VMEM(values.shape, BF16),
            pltpu.VMEM(queries.shape, BF16),
            block, block, block, block, block, block, total, total,
            pltpu.VMEM((ROWS + HALF, HALF), F32),
            pltpu.VMEM((HALF, HALF), F32),
            pltpu.SMEM(document_lengths.shape, jnp.int32),
            pltpu.SemaphoreType.DMA,
            pltpu.SemaphoreType.DMA((4, GROUPS)),
            pltpu.SemaphoreType.DMA((4, GROUPS)),
            pltpu.SemaphoreType.DMA((4, GROUPS)),
        ],
        compiler_params=pltpu.CompilerParams(
            collective_id=0, has_side_effects=True, vmem_limit_bytes=54 << 20
        ),
        name="packed_attention",
    )(document_lengths, queries, keys, values, output_gradient)


def solution(mesh):
    rows = P(("seq", "head"), None)
    return jax.shard_map(
        body,
        mesh=mesh,
        in_specs=(rows, rows, rows, rows, P()),
        out_specs=(rows, rows, rows, rows),
        check_vma=False,
    )
```

```python
import functools
import math

import jax
import jax.numpy as jnp
from jax import lax
from jax.experimental import pallas as pl
from jax.experimental.pallas import tpu as pltpu
from jax.sharding import PartitionSpec as P

QUERY_HEADS = 40
GROUPS = 8
RATIO = QUERY_HEADS // GROUPS
WIDTH = 128
WIDE = RATIO * WIDTH
ROWS = 256
HALF = 128
DOCS = 16
NEG = -1e30
SCALE = 1.0 / math.sqrt(WIDTH)
TO_EXP2 = SCALE * math.log2(math.e)
MESH = pl.DeviceIdType.MESH
F32 = jnp.float32
BF16 = jnp.bfloat16


def dot_nt(a, b):
    return lax.dot_general(a, b, (((1,), (1,)), ((), ())), preferred_element_type=F32)


def dot_nn(a, b):
    return jnp.dot(a, b, preferred_element_type=F32)


def stacked(ref, row, group):
    return jnp.concatenate(
        [
            ref[pl.ds(row, HALF), pl.ds(pl.multiple_of(group * WIDE + h * WIDTH, WIDTH), WIDTH)]
            for h in range(RATIO)
        ],
        axis=0,
    )


def columns(group):
    return pl.ds(pl.multiple_of(group * WIDTH, WIDTH), WIDTH)


def probabilities(keys, queries, bias):
    logits = dot_nt(keys, queries) * TO_EXP2 + jnp.concatenate([bias] * RATIO, axis=1)
    weights = jnp.exp2(logits - jnp.max(logits, axis=0, keepdims=True))
    return weights * (1.0 / jnp.sum(weights, axis=0, keepdims=True))


def score_gradient(probs, values, grads):
    dprobs = dot_nt(values, grads)
    delta = jnp.sum(probs * dprobs, axis=0, keepdims=True)
    return (probs * (dprobs - delta)).astype(BF16)


def put_heads(ref, row, group, transposed):
    for h in range(RATIO):
        block = transposed[:, h * WIDTH : (h + 1) * WIDTH].T
        where = pl.ds(pl.multiple_of(group * WIDE + h * WIDTH, WIDTH), WIDTH)
        ref[pl.ds(row, HALF), where] = block.astype(BF16)


def mask_bias(lengths, block, first_query, first_key, keys):
    query = first_query + lax.broadcasted_iota(jnp.int32, (1, HALF), 1)
    start = jnp.int32(0)
    doc_start = jnp.zeros((1, HALF), jnp.int32)
    for d in range(DOCS):
        doc_start = jnp.where(query >= start, start, doc_start)
        start = start + lengths[d, block]
    key = first_key + lax.broadcasted_iota(jnp.int32, (keys, HALF), 0)
    return jnp.where((key >= doc_start) & (key <= query), 0.0, NEG).astype(F32)


def kernel(
    lengths_hbm, q_hbm, k_hbm, v_hbm, g_hbm,
    o_out, dq_out, dk_out, dv_out,
    q_own, k_own, v_own, g_own,
    k_far, v_far, dk_send, dv_send, dk_far, dv_far, dk_sum, dv_sum,
    bias_a, bias_b, lengths, lengths_sem, load_sem, send_sem, recv_sem,
):
    seq = lax.axis_index("seq")
    head = lax.axis_index("head")
    partner = (seq, 1 - head)
    barrier = pltpu.get_barrier_semaphore()
    pl.semaphore_signal(barrier, inc=1, device_id=partner, device_id_type=MESH)

    lengths_copy = pltpu.make_async_copy(lengths_hbm, lengths, lengths_sem)
    lengths_copy.start()

    def loads(g):
        wide = pl.ds(pl.multiple_of(g * WIDE, WIDTH), WIDE)
        return [
            pltpu.make_async_copy(src.at[:, where], dst.at[:, where], load_sem.at[i, g])
            for i, (src, dst, where) in enumerate(
                (
                    (k_hbm, k_own, columns(g)),
                    (q_hbm, q_own, wide),
                    (g_hbm, g_own, wide),
                    (v_hbm, v_own, columns(g)),
                )
            )
        ]

    def far(i, g):
        src, dst = (
            (k_hbm.at[:, columns(g)], k_far.at[g]),
            (v_hbm.at[:, columns(g)], v_far.at[g]),
            (dv_send.at[g], dv_far.at[g]),
            (dk_send.at[g], dk_far.at[g]),
        )[i]
        return pltpu.make_async_remote_copy(
            src_ref=src,
            dst_ref=dst,
            send_sem=send_sem.at[i, g],
            recv_sem=recv_sem.at[i, g],
            device_id=partner,
            device_id_type=MESH,
        )

    def start_loads(g, _):
        for copy in loads(g):
            copy.start()
        return 0

    lax.fori_loop(0, GROUPS, start_loads, 0)
    lengths_copy.wait()
    pl.semaphore_wait(barrier, 1)

    @pl.when(head == 0)
    def _():
        def send(g, _):
            far(0, g).start()
            far(1, g).start()
            return 0

        lax.fori_loop(0, GROUPS, send, 0)
        bias_a[0:ROWS] = mask_bias(lengths, seq, HALF, 0, ROWS)
        bias_b[...] = mask_bias(lengths, seq, 0, 0, HALF)

        def local(g, _):
            for copy in loads(g):
                copy.wait()
            for row, keys, bias in ((HALF, ROWS, bias_a), (0, HALF, bias_b)):
                kk = k_own[0:keys, columns(g)]
                vv = v_own[0:keys, columns(g)]
                qq = stacked(q_own, row, g)
                gg = stacked(g_own, row, g)
                probs = probabilities(kk, qq, bias[0:keys])
                rounded = probs.astype(BF16)
                dscores = score_gradient(probs, vv, gg)
                dv = dot_nn(rounded, gg)
                dk = dot_nn(dscores, qq)
                if row:
                    dv_sum[g] = dv
                    dk_sum[g] = dk
                else:
                    dv_sum[g, 0:HALF] += dv
                    dk_sum[g, 0:HALF] += dk
                put_heads(o_out, row, g, dot_nn(vv.T, rounded))
                put_heads(dq_out, row, g, dot_nn(kk.T, dscores) * SCALE)
            return 0

        lax.fori_loop(0, GROUPS, local, 0)

        def finish(g, _):
            far(2, g).wait_recv()
            dv_out[:, columns(g)] = (dv_sum[g] + dv_far[g].astype(F32)).astype(BF16)
            far(3, g).wait_recv()
            dk_out[:, columns(g)] = (dk_sum[g] * SCALE + dk_far[g].astype(F32)).astype(BF16)
            return 0

        lax.fori_loop(0, GROUPS, finish, 0)

        def drain(g, _):
            far(0, g).wait_send()
            far(1, g).wait_send()
            return 0

        lax.fori_loop(0, GROUPS, drain, 0)

    @pl.when(head == 1)
    def _():
        bias_a[...] = mask_bias(lengths, seq, ROWS, 0, ROWS + HALF)
        bias_b[...] = mask_bias(lengths, seq, ROWS + HALF, ROWS + HALF, HALF)

        def work(g, _):
            for copy in loads(g):
                copy.wait()
            kk = k_own[HALF:ROWS, columns(g)]
            vv = v_own[HALF:ROWS, columns(g)]
            qq = stacked(q_own, HALF, g)
            gg = stacked(g_own, HALF, g)
            probs = probabilities(kk, qq, bias_b[...])
            rounded = probs.astype(BF16)
            dscores = score_gradient(probs, vv, gg)
            dv_out[HALF:ROWS, columns(g)] = dot_nn(rounded, gg).astype(BF16)
            dk_out[HALF:ROWS, columns(g)] = (dot_nn(dscores, qq) * SCALE).astype(BF16)
            put_heads(o_out, HALF, g, dot_nn(vv.T, rounded))
            put_heads(dq_out, HALF, g, dot_nn(kk.T, dscores) * SCALE)

            far(0, g).wait_recv()
            kk = jnp.concatenate([k_far[g], k_own[0:HALF, columns(g)]], axis=0)
            qq = stacked(q_own, 0, g)
            gg = stacked(g_own, 0, g)
            probs = probabilities(kk, qq, bias_a[...])
            rounded = probs.astype(BF16)
            dv = dot_nn(rounded, gg).astype(BF16)
            dv_send[g] = dv[0:ROWS]
            far(2, g).start()
            dv_out[0:HALF, columns(g)] = dv[ROWS:]
            far(1, g).wait_recv()
            vv = jnp.concatenate([v_far[g], v_own[0:HALF, columns(g)]], axis=0)
            dscores = score_gradient(probs, vv, gg)
            dk = (dot_nn(dscores, qq) * SCALE).astype(BF16)
            dk_send[g] = dk[0:ROWS]
            far(3, g).start()
            dk_out[0:HALF, columns(g)] = dk[ROWS:]
            put_heads(o_out, 0, g, dot_nn(vv.T, rounded))
            put_heads(dq_out, 0, g, dot_nn(kk.T, dscores) * SCALE)
            return 0

        lax.fori_loop(0, GROUPS, work, 0)

        def drain(g, _):
            far(2, g).wait_send()
            far(3, g).wait_send()
            return 0

        lax.fori_loop(0, GROUPS, drain, 0)


def store_kernel(*refs):
    count = len(refs) // 2
    copies = [
        pltpu.make_async_copy(refs[i], refs[count + i], refs[-1].at[i]) for i in range(count)
    ]
    for copy in copies:
        copy.start()
    for copy in copies:
        copy.wait()


def body(queries, keys, values, output_gradient, document_lengths):
    hbm = pl.BlockSpec(memory_space=pl.ANY)
    block = pltpu.VMEM((GROUPS, ROWS, WIDTH), BF16)
    total = pltpu.VMEM((GROUPS, ROWS, WIDTH), F32)
    results = pl.pallas_call(
        kernel,
        out_shape=[pltpu.VMEM(x.shape, BF16) for x in (queries, queries, keys, values)],
        in_specs=[hbm] * 5,
        scratch_shapes=[
            pltpu.VMEM(queries.shape, BF16),
            pltpu.VMEM(keys.shape, BF16),
            pltpu.VMEM(values.shape, BF16),
            pltpu.VMEM(queries.shape, BF16),
            block, block, block, block, block, block, total, total,
            pltpu.VMEM((ROWS + HALF, HALF), F32),
            pltpu.VMEM((HALF, HALF), F32),
            pltpu.SMEM(document_lengths.shape[::-1], jnp.int32),
            pltpu.SemaphoreType.DMA,
            pltpu.SemaphoreType.DMA((4, GROUPS)),
            pltpu.SemaphoreType.DMA((4, GROUPS)),
            pltpu.SemaphoreType.DMA((4, GROUPS)),
        ],
        compiler_params=pltpu.CompilerParams(
            collective_id=0, has_side_effects=True, vmem_limit_bytes=54 << 20
        ),
        name="packed_attention",
    )(document_lengths.T, queries, keys, values, output_gradient)
    return pl.pallas_call(
        store_kernel,
        out_shape=[jax.ShapeDtypeStruct(x.shape, BF16) for x in results],
        in_specs=[pl.BlockSpec(memory_space=pltpu.VMEM)] * len(results),
        out_specs=[hbm] * len(results),
        scratch_shapes=[pltpu.SemaphoreType.DMA((len(results),))],
        compiler_params=pltpu.CompilerParams(vmem_limit_bytes=16 << 20),
        name="store_results",
    )(*[pltpu.with_memory_space_constraint(x, pltpu.VMEM) for x in results])


def solution(mesh):
    rows = P(("seq", "head"), None)
    return jax.shard_map(
        body,
        mesh=mesh,
        in_specs=(rows, rows, rows, rows, P()),
        out_specs=(rows, rows, rows, rows),
        check_vma=False,
    )
```

```python
import functools
import math

import jax
import jax.numpy as jnp
from jax import lax
from jax.experimental import pallas as pl
from jax.experimental.pallas import tpu as pltpu
from jax.sharding import PartitionSpec as P

QUERY_HEADS = 40
GROUPS = 8
RATIO = QUERY_HEADS // GROUPS
WIDTH = 128
WIDE = RATIO * WIDTH
ROWS = 256
HALF = 128
DOCS = 16
NEG = -1e30
SCALE = 1.0 / math.sqrt(WIDTH)
TO_EXP2 = SCALE * math.log2(math.e)
LEAD = 1
MESH = pl.DeviceIdType.MESH
F32 = jnp.float32
BF16 = jnp.bfloat16


def dot_nt(a, b):
    return lax.dot_general(a, b, (((1,), (1,)), ((), ())), preferred_element_type=F32)


def dot_nn(a, b):
    return jnp.dot(a, b, preferred_element_type=F32)


def stacked(ref, row, group):
    return jnp.concatenate(
        [
            ref[pl.ds(row, HALF), pl.ds(pl.multiple_of(group * WIDE + h * WIDTH, WIDTH), WIDTH)]
            for h in range(RATIO)
        ],
        axis=0,
    )


def columns(group):
    return pl.ds(pl.multiple_of(group * WIDTH, WIDTH), WIDTH)


PARTS = [slice(0, 256), slice(256, 512), slice(512, 640)]


def wide(parts):
    return jnp.concatenate([x.astype(BF16) for x in parts], axis=1)


def logits(keys, queries, bias):
    heads = queries.shape[0] // WIDTH
    return dot_nt(keys, queries) * TO_EXP2 + jnp.concatenate([bias] * heads, axis=1)


def probabilities(keys, queries, bias):
    logits = dot_nt(keys, queries) * TO_EXP2 + jnp.concatenate([bias] * RATIO, axis=1)
    weights = jnp.exp2(logits - jnp.max(logits, axis=0, keepdims=True))
    return weights * (1.0 / jnp.sum(weights, axis=0, keepdims=True))


def score_gradient(probs, values, grads):
    dprobs = dot_nt(values, grads)
    delta = jnp.sum(probs * dprobs, axis=0, keepdims=True)
    return (probs * (dprobs - delta)).astype(BF16)


def put_heads(ref, row, group, transposed):
    for h in range(RATIO):
        block = transposed[:, h * WIDTH : (h + 1) * WIDTH].T
        where = pl.ds(pl.multiple_of(group * WIDE + h * WIDTH, WIDTH), WIDTH)
        ref[pl.ds(row, HALF), where] = block.astype(BF16)


def mask_bias(lengths, block, first_query, first_key, keys):
    query = first_query + lax.broadcasted_iota(jnp.int32, (1, HALF), 1)
    start = jnp.int32(0)
    doc_start = jnp.zeros((1, HALF), jnp.int32)
    for d in range(DOCS):
        doc_start = jnp.where(query >= start, start, doc_start)
        start = start + lengths[d, block]
    key = first_key + lax.broadcasted_iota(jnp.int32, (keys, HALF), 0)
    return jnp.where((key >= doc_start) & (key <= query), 0.0, NEG).astype(F32)


def kernel(
    lengths_hbm, q_hbm, k_hbm, v_hbm, g_hbm,
    o_out, dq_out, dk_out, dv_out,
    q_own, k_own, v_own, g_own,
    k_far, v_far, dk_send, dv_send, dk_far, dv_far, dk_sum, dv_sum,
    bias_a, bias_b, lengths, lengths_sem, load_sem, send_sem, recv_sem,
):
    seq = lax.axis_index("seq")
    head = lax.axis_index("head")
    core = lax.rem(seq, 2)
    partner = (seq, 1 - head)
    barrier = pltpu.get_barrier_semaphore()
    pl.semaphore_signal(barrier, inc=1, device_id=partner, device_id_type=MESH)

    lengths_copy = pltpu.make_async_copy(lengths_hbm, lengths, lengths_sem)

    def load(i, g):
        src, dst = ((k_hbm, k_own), (v_hbm, v_own), (q_hbm, q_own), (g_hbm, g_own))[i]
        where = columns(g) if i < 2 else pl.ds(pl.multiple_of(g * WIDE, WIDTH), WIDE)
        return pltpu.make_async_copy(src.at[:, where], dst.at[:, where], load_sem.at[i, g])

    def far(i, g):
        src, dst = (
            (k_own.at[:, columns(g)], k_far.at[g]),
            (v_own.at[:, columns(g)], v_far.at[g]),
            (dv_send.at[g], dv_far.at[g]),
            (dk_send.at[g], dk_far.at[g]),
        )[i]
        return pltpu.make_async_remote_copy(
            src_ref=src,
            dst_ref=dst,
            send_sem=send_sem.at[i, g],
            recv_sem=recv_sem.at[i, g],
            device_id=partner,
            device_id_type=MESH,
        )

    def start_key_loads(g, _):
        load(0, g).start()
        load(1, g).start()
        return 0

    def start_query_loads(g, _):
        load(2, g).start()
        load(3, g).start()
        return 0

    lax.fori_loop(0, GROUPS, start_key_loads, 0)

    @pl.when(head == 0)
    def _():
        def send(g, _):
            load(0, g).wait()
            far(0, g).start()
            load(1, g).wait()
            far(1, g).start()
            return 0

        def drain(g, _):
            far(0, g).wait_send()
            far(1, g).wait_send()
            return 0

        pl.semaphore_wait(barrier, 1)
        lax.fori_loop(0, LEAD, send, 0)

        @pl.when(core == 1)
        def _():
            lax.fori_loop(0, LEAD, drain, 0)

        lax.fori_loop(LEAD, GROUPS, send, 0)
        lengths_copy.start()
        lax.fori_loop(0, GROUPS, start_query_loads, 0)
        lengths_copy.wait()
        bias_a[0:ROWS] = mask_bias(lengths, seq, HALF, 0, ROWS)
        bias_b[...] = mask_bias(lengths, seq, 0, 0, HALF)

        def local(g, _):
            load(2, g).wait()
            load(3, g).wait()
            for row, keys, bias in ((HALF, ROWS, bias_a), (0, HALF, bias_b)):
                kk = k_own[0:keys, columns(g)]
                vv = v_own[0:keys, columns(g)]
                qq = stacked(q_own, row, g)
                gg = stacked(g_own, row, g)
                probs = probabilities(kk, qq, bias[0:keys])
                rounded = probs.astype(BF16)
                dscores = score_gradient(probs, vv, gg)
                dv = dot_nn(rounded, gg)
                dk = dot_nn(dscores, qq)
                if row:
                    dv_sum[g] = dv
                    dk_sum[g] = dk
                else:
                    dv_sum[g, 0:HALF] += dv
                    dk_sum[g, 0:HALF] += dk
                put_heads(o_out, row, g, dot_nn(vv.T, rounded))
                put_heads(dq_out, row, g, dot_nn(kk.T, dscores) * SCALE)
            return 0

        lax.fori_loop(0, GROUPS, local, 0)

        def finish(g, _):
            far(2, g).wait_recv()
            dv_out[:, columns(g)] = (dv_sum[g] + dv_far[g].astype(F32)).astype(BF16)
            far(3, g).wait_recv()
            dk_out[:, columns(g)] = (dk_sum[g] * SCALE + dk_far[g].astype(F32)).astype(BF16)
            return 0

        lax.fori_loop(0, GROUPS - 1, finish, 0)
        lax.fori_loop(jnp.where(core == 1, LEAD, 0), GROUPS, drain, 0)
        finish(GROUPS - 1, 0)

    @pl.when(head == 1)
    def _():
        lengths_copy.start()
        lax.fori_loop(0, GROUPS, start_query_loads, 0)
        pl.semaphore_wait(barrier, 1)
        lengths_copy.wait()
        bias_a[...] = mask_bias(lengths, seq, ROWS, 0, ROWS + HALF)
        bias_b[...] = mask_bias(lengths, seq, ROWS + HALF, ROWS + HALF, HALF)

        def work(g, _):
            for i in range(4):
                load(i, g).wait()
            kk = k_own[HALF:ROWS, columns(g)]
            vv = v_own[HALF:ROWS, columns(g)]
            qq = stacked(q_own, HALF, g)
            gg = stacked(g_own, HALF, g)
            probs = probabilities(kk, qq, bias_b[...])
            rounded = probs.astype(BF16)
            dscores = score_gradient(probs, vv, gg)
            dv_out[HALF:ROWS, columns(g)] = dot_nn(rounded, gg).astype(BF16)
            dk_out[HALF:ROWS, columns(g)] = (dot_nn(dscores, qq) * SCALE).astype(BF16)
            put_heads(o_out, HALF, g, dot_nn(vv.T, rounded))
            put_heads(dq_out, HALF, g, dot_nn(kk.T, dscores) * SCALE)

            k_near = k_own[0:HALF, columns(g)]
            v_near = v_own[0:HALF, columns(g)]
            qq = stacked(q_own, 0, g)
            gg = stacked(g_own, 0, g)
            bias_far, bias_near = bias_a[0:ROWS], bias_a[ROWS:]
            near_logits = [logits(k_near, qq[part], bias_near) for part in PARTS]
            near_top = [jnp.max(x, axis=0, keepdims=True) for x in near_logits]
            near_dprobs = [dot_nt(v_near, gg[part]) for part in PARTS]

            far(0, g).wait_recv()
            k_there = k_far[g]
            probs_far, probs_near, near_sum = [], [], []
            for n, part in enumerate(PARTS):
                far_logits = logits(k_there, qq[part], bias_far)
                top = jnp.maximum(near_top[n], jnp.max(far_logits, axis=0, keepdims=True))
                weights_far = jnp.exp2(far_logits - top)
                weights_near = jnp.exp2(near_logits[n] - top)
                total = jnp.sum(weights_far, axis=0, keepdims=True)
                total += jnp.sum(weights_near, axis=0, keepdims=True)
                probs_far.append(weights_far * (1.0 / total))
                probs_near.append(weights_near * (1.0 / total))
            rounded_far = wide(probs_far)
            rounded_near = wide(probs_near)
            dv_send[g] = dot_nn(rounded_far, gg).astype(BF16)
            far(2, g).start()
            near_sum = [
                jnp.sum(p * d, axis=0, keepdims=True) for p, d in zip(probs_near, near_dprobs)
            ]

            far(1, g).wait_recv()
            v_there = v_far[g]
            dscores_far, deltas = [], []
            for n, part in enumerate(PARTS):
                dprobs = dot_nt(v_there, gg[part])
                delta = near_sum[n] + jnp.sum(probs_far[n] * dprobs, axis=0, keepdims=True)
                dscores_far.append(probs_far[n] * (dprobs - delta))
                deltas.append(delta)
            dscores_far = wide(dscores_far)
            dk_send[g] = (dot_nn(dscores_far, qq) * SCALE).astype(BF16)
            far(3, g).start()
            dscores_near = wide(
                [p * (d - delta) for p, d, delta in zip(probs_near, near_dprobs, deltas)]
            )
            dv_out[0:HALF, columns(g)] = dot_nn(rounded_near, gg).astype(BF16)
            dk_out[0:HALF, columns(g)] = (dot_nn(dscores_near, qq) * SCALE).astype(BF16)
            vv = jnp.concatenate([v_there, v_near], axis=0)
            kk = jnp.concatenate([k_there, k_near], axis=0)
            rounded = jnp.concatenate([rounded_far, rounded_near], axis=0)
            dscores = jnp.concatenate([dscores_far, dscores_near], axis=0)
            put_heads(o_out, 0, g, dot_nn(vv.T, rounded))
            put_heads(dq_out, 0, g, dot_nn(kk.T, dscores) * SCALE)
            return 0

        lax.fori_loop(0, GROUPS, work, 0)

        def drain(g, _):
            far(2, g).wait_send()
            far(3, g).wait_send()
            return 0

        lax.fori_loop(0, GROUPS, drain, 0)


def store_kernel(*refs):
    count = len(refs) // 2
    copies = [
        pltpu.make_async_copy(refs[i], refs[count + i], refs[-1].at[i]) for i in range(count)
    ]
    for copy in copies:
        copy.start()
    for copy in copies:
        copy.wait()


def body(queries, keys, values, output_gradient, document_lengths):
    hbm = pl.BlockSpec(memory_space=pl.ANY)
    block = pltpu.VMEM((GROUPS, ROWS, WIDTH), BF16)
    total = pltpu.VMEM((GROUPS, ROWS, WIDTH), F32)
    results = pl.pallas_call(
        kernel,
        out_shape=[pltpu.VMEM(x.shape, BF16) for x in (queries, queries, keys, values)],
        in_specs=[hbm] * 5,
        scratch_shapes=[
            pltpu.VMEM(queries.shape, BF16),
            pltpu.VMEM(keys.shape, BF16),
            pltpu.VMEM(values.shape, BF16),
            pltpu.VMEM(queries.shape, BF16),
            block, block, block, block, block, block, total, total,
            pltpu.VMEM((ROWS + HALF, HALF), F32),
            pltpu.VMEM((HALF, HALF), F32),
            pltpu.SMEM(document_lengths.shape[::-1], jnp.int32),
            pltpu.SemaphoreType.DMA,
            pltpu.SemaphoreType.DMA((4, GROUPS)),
            pltpu.SemaphoreType.DMA((4, GROUPS)),
            pltpu.SemaphoreType.DMA((4, GROUPS)),
        ],
        compiler_params=pltpu.CompilerParams(
            collective_id=0, has_side_effects=True, vmem_limit_bytes=54 << 20
        ),
        name="packed_attention",
    )(document_lengths.T, queries, keys, values, output_gradient)
    return pl.pallas_call(
        store_kernel,
        out_shape=[jax.ShapeDtypeStruct(x.shape, BF16) for x in results],
        in_specs=[pl.BlockSpec(memory_space=pltpu.VMEM)] * len(results),
        out_specs=[hbm] * len(results),
        scratch_shapes=[pltpu.SemaphoreType.DMA((len(results),))],
        compiler_params=pltpu.CompilerParams(vmem_limit_bytes=16 << 20),
        name="store_results",
    )(*[pltpu.with_memory_space_constraint(x, pltpu.VMEM) for x in results])


def solution(mesh):
    rows = P(("seq", "head"), None)
    return jax.shard_map(
        body,
        mesh=mesh,
        in_specs=(rows, rows, rows, rows, P()),
        out_specs=(rows, rows, rows, rows),
        check_vma=False,
    )
```

```python
import functools
import math

import jax
import jax.numpy as jnp
from jax import lax
from jax.experimental import pallas as pl
from jax.experimental.pallas import tpu as pltpu
from jax.sharding import PartitionSpec as P

QUERY_HEADS = 40
GROUPS = 8
RATIO = QUERY_HEADS // GROUPS
WIDTH = 128
WIDE = RATIO * WIDTH
ROWS = 256
HALF = 128
DOCS = 16
NEG = -1e30
SCALE = 1.0 / math.sqrt(WIDTH)
TO_EXP2 = SCALE * math.log2(math.e)
MESH = pl.DeviceIdType.MESH
F32 = jnp.float32
BF16 = jnp.bfloat16


def dot_nt(a, b):
    return lax.dot_general(a, b, (((1,), (1,)), ((), ())), preferred_element_type=F32)


def dot_nn(a, b):
    return jnp.dot(a, b, preferred_element_type=F32)


def stacked(ref, row, group):
    return jnp.concatenate(
        [
            ref[pl.ds(row, HALF), pl.ds(pl.multiple_of(group * WIDE + h * WIDTH, WIDTH), WIDTH)]
            for h in range(RATIO)
        ],
        axis=0,
    )


def columns(group):
    return pl.ds(pl.multiple_of(group * WIDTH, WIDTH), WIDTH)


def logits(keys, queries, bias):
    return dot_nt(keys, queries) * TO_EXP2 + jnp.concatenate([bias] * RATIO, axis=1)


def probabilities(keys, queries, bias):
    scaled = logits(keys, queries, bias)
    weights = jnp.exp2(scaled - jnp.max(scaled, axis=0, keepdims=True))
    return weights * (1.0 / jnp.sum(weights, axis=0, keepdims=True))


def score_gradient(probs, values, grads):
    dprobs = dot_nt(values, grads)
    delta = jnp.sum(probs * dprobs, axis=0, keepdims=True)
    return (probs * (dprobs - delta)).astype(BF16)


def put_heads(ref, row, group, transposed):
    for h in range(RATIO):
        block = transposed[:, h * WIDTH : (h + 1) * WIDTH].T
        where = pl.ds(pl.multiple_of(group * WIDE + h * WIDTH, WIDTH), WIDTH)
        ref[pl.ds(row, HALF), where] = block.astype(BF16)


def mask_bias(lengths, block, first_query, first_key, keys):
    query = first_query + lax.broadcasted_iota(jnp.int32, (1, HALF), 1)
    start = jnp.int32(0)
    doc_start = jnp.zeros((1, HALF), jnp.int32)
    for d in range(DOCS):
        doc_start = jnp.where(query >= start, start, doc_start)
        start = start + lengths[d, block]
    key = first_key + lax.broadcasted_iota(jnp.int32, (keys, HALF), 0)
    return jnp.where((key >= doc_start) & (key <= query), 0.0, NEG).astype(F32)


def kernel(
    lengths_hbm, q_hbm, k_hbm, v_hbm, g_hbm,
    o_out, dq_out, dk_out, dv_out,
    q_own, k_own, v_own, g_own,
    kv_far, dkv_send, dkv_far, dk_sum, dv_sum,
    bias_a, bias_b, lengths, load_sem, send_sem, recv_sem,
):
    seq = lax.axis_index("seq")
    head = lax.axis_index("head")
    core = lax.rem(seq, 2)
    partner = (seq, 1 - head)
    barrier = pltpu.get_barrier_semaphore()
    pl.semaphore_signal(barrier, inc=1, device_id=partner, device_id_type=MESH)

    def load(i):
        src, dst = (
            (k_hbm, k_own), (v_hbm, v_own), (q_hbm, q_own), (g_hbm, g_own), (lengths_hbm, lengths)
        )[i]
        return pltpu.make_async_copy(src, dst, load_sem.at[i])

    def send(src, dst, sent, landed):
        return pltpu.make_async_remote_copy(
            src_ref=src,
            dst_ref=dst,
            send_sem=send_sem.at[sent],
            recv_sem=recv_sem.at[landed],
            device_id=partner,
            device_id_type=MESH,
        )

    def far(i, g, sent=1):
        at = 2 * g + i % 2
        if i < 2:
            return send((k_own, v_own)[i].at[:, columns(g)], kv_far.at[at], sent, at)
        return send(dkv_send.at[at], dkv_far.at[at], sent, at)

    def wait_sent(sent, blocks):
        every = kv_far.at[0:blocks]
        send(every, every, sent, 0).wait_send()

    load(0).start()
    load(1).start()

    @pl.when(head == 0)
    def _():
        pl.semaphore_wait(barrier, 1)
        load(0).wait()
        far(0, 0, 0).start()
        load(1).wait()
        far(1, 0, 0).start()

        @pl.when(core == 1)
        def _():
            wait_sent(0, 2)

        def send_group(g, _):
            far(0, g).start()
            far(1, g).start()
            return 0

        lax.fori_loop(1, GROUPS, send_group, 0)
        load(4).start()
        load(2).start()
        load(3).start()
        load(4).wait()
        bias_a[0:ROWS] = mask_bias(lengths, seq, HALF, 0, ROWS)
        bias_b[...] = mask_bias(lengths, seq, 0, 0, HALF)
        load(2).wait()
        load(3).wait()

        def local(g, _):
            for row, keys, bias in ((HALF, ROWS, bias_a), (0, HALF, bias_b)):
                kk = k_own[0:keys, columns(g)]
                vv = v_own[0:keys, columns(g)]
                qq = stacked(q_own, row, g)
                gg = stacked(g_own, row, g)
                probs = probabilities(kk, qq, bias[0:keys])
                rounded = probs.astype(BF16)
                dscores = score_gradient(probs, vv, gg)
                dv = dot_nn(rounded, gg)
                dk = dot_nn(dscores, qq)
                if row:
                    dv_sum[g] = dv
                    dk_sum[g] = dk
                else:
                    dv_sum[g, 0:HALF] += dv
                    dk_sum[g, 0:HALF] += dk
                put_heads(o_out, row, g, dot_nn(vv.T, rounded))
                put_heads(dq_out, row, g, dot_nn(kk.T, dscores) * SCALE)
            return 0

        lax.fori_loop(0, GROUPS, local, 0)

        def finish(g, _):
            far(2, g).wait_recv()
            dv_out[:, columns(g)] = (dv_sum[g] + dkv_far[2 * g].astype(F32)).astype(BF16)
            far(3, g).wait_recv()
            dk_out[:, columns(g)] = (dk_sum[g] * SCALE + dkv_far[2 * g + 1].astype(F32)).astype(BF16)
            return 0

        lax.fori_loop(0, GROUPS - 1, finish, 0)

        @pl.when(core == 0)
        def _():
            wait_sent(0, 2)

        wait_sent(1, 2 * GROUPS - 2)
        finish(GROUPS - 1, 0)

    @pl.when(head == 1)
    def _():
        load(4).start()
        load(2).start()
        load(3).start()
        pl.semaphore_wait(barrier, 1)
        load(4).wait()
        bias_a[...] = mask_bias(lengths, seq, ROWS, 0, ROWS + HALF)
        bias_b[...] = mask_bias(lengths, seq, ROWS + HALF, ROWS + HALF, HALF)
        for i in range(4):
            load(i).wait()

        def work(g, _):
            kk = k_own[HALF:ROWS, columns(g)]
            vv = v_own[HALF:ROWS, columns(g)]
            qq = stacked(q_own, HALF, g)
            gg = stacked(g_own, HALF, g)
            probs = probabilities(kk, qq, bias_b[...])
            rounded = probs.astype(BF16)
            dscores = score_gradient(probs, vv, gg)
            dv_out[HALF:ROWS, columns(g)] = dot_nn(rounded, gg).astype(BF16)
            dk_out[HALF:ROWS, columns(g)] = (dot_nn(dscores, qq) * SCALE).astype(BF16)
            put_heads(o_out, HALF, g, dot_nn(vv.T, rounded))
            put_heads(dq_out, HALF, g, dot_nn(kk.T, dscores) * SCALE)

            k_near = k_own[0:HALF, columns(g)]
            v_near = v_own[0:HALF, columns(g)]
            qq = stacked(q_own, 0, g)
            gg = stacked(g_own, 0, g)
            near_logits = logits(k_near, qq, bias_a[ROWS:])
            near_top = jnp.max(near_logits, axis=0, keepdims=True)
            near_dprobs = dot_nt(v_near, gg)

            far(0, g).wait_recv()
            k_there = kv_far[2 * g]
            far_logits = logits(k_there, qq, bias_a[0:ROWS])
            top = jnp.maximum(near_top, jnp.max(far_logits, axis=0, keepdims=True))
            probs_far = jnp.exp2(far_logits - top)
            probs_near = jnp.exp2(near_logits - top)
            total = jnp.sum(probs_far, axis=0, keepdims=True)
            total += jnp.sum(probs_near, axis=0, keepdims=True)
            probs_far *= 1.0 / total
            probs_near *= 1.0 / total
            rounded_far = probs_far.astype(BF16)
            rounded_near = probs_near.astype(BF16)
            dkv_send[2 * g] = dot_nn(rounded_far, gg).astype(BF16)
            far(2, g).start()
            near_sum = jnp.sum(probs_near * near_dprobs, axis=0, keepdims=True)

            far(1, g).wait_recv()
            v_there = kv_far[2 * g + 1]
            dprobs = dot_nt(v_there, gg)
            delta = near_sum + jnp.sum(probs_far * dprobs, axis=0, keepdims=True)
            dscores_far = (probs_far * (dprobs - delta)).astype(BF16)
            dkv_send[2 * g + 1] = (dot_nn(dscores_far, qq) * SCALE).astype(BF16)
            far(3, g).start()
            dscores_near = (probs_near * (near_dprobs - delta)).astype(BF16)
            dv_out[0:HALF, columns(g)] = dot_nn(rounded_near, gg).astype(BF16)
            dk_out[0:HALF, columns(g)] = (dot_nn(dscores_near, qq) * SCALE).astype(BF16)
            vv = jnp.concatenate([v_there, v_near], axis=0)
            kk = jnp.concatenate([k_there, k_near], axis=0)
            rounded = jnp.concatenate([rounded_far, rounded_near], axis=0)
            dscores = jnp.concatenate([dscores_far, dscores_near], axis=0)
            put_heads(o_out, 0, g, dot_nn(vv.T, rounded))
            put_heads(dq_out, 0, g, dot_nn(kk.T, dscores) * SCALE)
            return 0

        lax.fori_loop(0, GROUPS, work, 0)

        wait_sent(1, 2 * GROUPS)


def store_kernel(*refs):
    count = len(refs) // 2
    copies = [
        pltpu.make_async_copy(refs[i], refs[count + i], refs[-1].at[i]) for i in range(count)
    ]
    for copy in copies:
        copy.start()
    for copy in copies:
        copy.wait()


def body(queries, keys, values, output_gradient, document_lengths):
    hbm = pl.BlockSpec(memory_space=pl.ANY)
    blocks = pltpu.VMEM((2 * GROUPS, ROWS, WIDTH), BF16)
    total = pltpu.VMEM((GROUPS, ROWS, WIDTH), F32)
    results = pl.pallas_call(
        kernel,
        out_shape=[pltpu.VMEM(x.shape, BF16) for x in (queries, queries, keys, values)],
        in_specs=[hbm] * 5,
        scratch_shapes=[
            pltpu.VMEM(queries.shape, BF16),
            pltpu.VMEM(keys.shape, BF16),
            pltpu.VMEM(values.shape, BF16),
            pltpu.VMEM(queries.shape, BF16),
            blocks, blocks, blocks, total, total,
            pltpu.VMEM((ROWS + HALF, HALF), F32),
            pltpu.VMEM((HALF, HALF), F32),
            pltpu.SMEM(document_lengths.shape[::-1], jnp.int32),
            pltpu.SemaphoreType.DMA((5,)),
            pltpu.SemaphoreType.DMA((2,)),
            pltpu.SemaphoreType.DMA((2 * GROUPS,)),
        ],
        compiler_params=pltpu.CompilerParams(
            collective_id=0, has_side_effects=True, vmem_limit_bytes=54 << 20
        ),
        name="packed_attention",
    )(document_lengths.T, queries, keys, values, output_gradient)
    return pl.pallas_call(
        store_kernel,
        out_shape=[jax.ShapeDtypeStruct(x.shape, BF16) for x in results],
        in_specs=[pl.BlockSpec(memory_space=pltpu.VMEM)] * len(results),
        out_specs=[hbm] * len(results),
        scratch_shapes=[pltpu.SemaphoreType.DMA((len(results),))],
        compiler_params=pltpu.CompilerParams(vmem_limit_bytes=16 << 20),
        name="store_results",
    )(*[pltpu.with_memory_space_constraint(x, pltpu.VMEM) for x in results])


def solution(mesh):
    rows = P(("seq", "head"), None)
    return jax.shard_map(
        body,
        mesh=mesh,
        in_specs=(rows, rows, rows, rows, P()),
        out_specs=(rows, rows, rows, rows),
        check_vma=False,
    )
```

```python
import functools
import math

import jax
import jax.numpy as jnp
from jax import lax
from jax.experimental import pallas as pl
from jax.experimental.pallas import tpu as pltpu
from jax.sharding import PartitionSpec as P

QUERY_HEADS = 40
GROUPS = 8
RATIO = QUERY_HEADS // GROUPS
WIDTH = 128
WIDE = RATIO * WIDTH
ROWS = 256
HALF = 128
DOCS = 16
NEG = -1e30
SCALE = 1.0 / math.sqrt(WIDTH)
TO_EXP2 = SCALE * math.log2(math.e)
MESH = pl.DeviceIdType.MESH
F32 = jnp.float32
BF16 = jnp.bfloat16


def dot_nt(a, b):
    return lax.dot_general(a, b, (((1,), (1,)), ((), ())), preferred_element_type=F32)


def dot_nn(a, b):
    return jnp.dot(a, b, preferred_element_type=F32)


def stacked(ref, row, group):
    return jnp.concatenate(
        [
            ref[pl.ds(row, HALF), columns(group * RATIO + h)]
            for h in range(RATIO)
        ],
        axis=0,
    )


def columns(group):
    if isinstance(group, int):
        return slice(group * WIDTH, (group + 1) * WIDTH)
    return pl.ds(pl.multiple_of(group * WIDTH, WIDTH), WIDTH)


def logits(keys, queries, bias):
    return dot_nt(keys, queries) * TO_EXP2 + jnp.concatenate([bias] * RATIO, axis=1)


def probabilities(keys, queries, bias):
    scaled = logits(keys, queries, bias)
    weights = jnp.exp2(scaled - jnp.max(scaled, axis=0, keepdims=True))
    return weights * (1.0 / jnp.sum(weights, axis=0, keepdims=True))


def score_gradient(probs, values, grads):
    dprobs = dot_nt(values, grads)
    delta = jnp.sum(probs * dprobs, axis=0, keepdims=True)
    return (probs * (dprobs - delta)).astype(BF16)


def put_heads(ref, row, group, transposed):
    for h in range(RATIO):
        block = transposed[:, h * WIDTH : (h + 1) * WIDTH].T
        ref[pl.ds(row, HALF), columns(group * RATIO + h)] = block.astype(BF16)


def mask_bias(lengths, block, first_query, first_key, keys):
    query = first_query + lax.broadcasted_iota(jnp.int32, (1, HALF), 1)
    start = jnp.int32(0)
    doc_start = jnp.zeros((1, HALF), jnp.int32)
    for d in range(DOCS):
        doc_start = jnp.where(query >= start, start, doc_start)
        start = start + lengths[d, block]
    key = first_key + lax.broadcasted_iota(jnp.int32, (keys, HALF), 0)
    return jnp.where((key >= doc_start) & (key <= query), 0.0, NEG).astype(F32)


def kernel(
    lengths_hbm, q_hbm, k_hbm, v_hbm, g_hbm,
    o_out, dq_out, dk_out, dv_out,
    q_own, k_own, v_own, g_own,
    kv_far, dkv_send, dkv_far, dk_sum, dv_sum,
    lent_wide, lent, given_wide, given,
    bias_a, bias_b, bias_lent, lengths, load_sem, send_sem, recv_sem,
):
    seq = lax.axis_index("seq")
    head = lax.axis_index("head")
    core = lax.rem(seq, 2)
    last = GROUPS - 1
    groups = jnp.where(core == 0, last, GROUPS)
    partner = (seq, 1 - head)
    barrier = pltpu.get_barrier_semaphore()
    pl.semaphore_signal(barrier, inc=1, device_id=partner, device_id_type=MESH)

    def load(i):
        src, dst = (
            (k_hbm, k_own), (v_hbm, v_own), (q_hbm, q_own), (g_hbm, g_own), (lengths_hbm, lengths)
        )[i]
        return pltpu.make_async_copy(src, dst, load_sem.at[i])

    def send(src, dst, sent, landed):
        return pltpu.make_async_remote_copy(
            src_ref=src,
            dst_ref=dst,
            send_sem=send_sem.at[sent],
            recv_sem=recv_sem.at[landed],
            device_id=partner,
            device_id_type=MESH,
        )

    def far(i, g, sent=1):
        at = 2 * g + i % 2
        if i < 2:
            return send((k_own, v_own)[i].at[:, columns(g)], kv_far.at[at], sent, at)
        return send(dkv_send.at[at], dkv_far.at[at], sent, at)

    def lend(i):
        rows, wide, narrow = slice(0, HALF), slice(last * WIDE, GROUPS * WIDE), columns(last)
        src = (q_hbm.at[rows, wide], g_hbm.at[rows, wide], k_hbm.at[rows, narrow], v_hbm.at[rows, narrow])
        dst = (lent_wide if i < 2 else lent).at[i % 2]
        return send(src[i], dst, 0, 2 * GROUPS - 2 + i)

    def give_back(i):
        src, dst = (given_wide, lent_wide) if i < 2 else (given, lent)
        return send(src.at[i % 2], dst.at[i % 2], 0, 2 * GROUPS - 2 + i)

    def wait_sent(sent, blocks):
        every = kv_far.at[0:blocks]
        send(every, every, sent, 0).wait_send()

    load(0).start()
    load(1).start()

    @pl.when(head == 0)
    def _():
        pl.semaphore_wait(barrier, 1)
        load(0).wait()
        far(0, 0, 0).start()
        load(1).wait()
        far(1, 0, 0).start()

        @pl.when(core == 1)
        def _():
            wait_sent(0, 2)

        def send_group(g, _):
            far(0, g).start()
            far(1, g).start()
            return 0

        lax.fori_loop(1, groups, send_group, 0)
        load(4).start()
        load(2).start()
        load(3).start()
        load(4).wait()
        bias_a[0:ROWS] = mask_bias(lengths, seq, HALF, 0, ROWS)
        bias_b[...] = mask_bias(lengths, seq, 0, 0, HALF)
        load(2).wait()
        load(3).wait()

        def local(g, _):
            for row, keys, bias in ((HALF, ROWS, bias_a), (0, HALF, bias_b)):
                kk = k_own[0:keys, columns(g)]
                vv = v_own[0:keys, columns(g)]
                qq = stacked(q_own, row, g)
                gg = stacked(g_own, row, g)
                probs = probabilities(kk, qq, bias[0:keys])
                rounded = probs.astype(BF16)
                dscores = score_gradient(probs, vv, gg)
                dv = dot_nn(rounded, gg)
                dk = dot_nn(dscores, qq)
                if row:
                    dv_sum[g] = dv
                    dk_sum[g] = dk
                else:
                    dv_sum[g, 0:HALF] += dv
                    dk_sum[g, 0:HALF] += dk
                put_heads(o_out, row, g, dot_nn(vv.T, rounded))
                put_heads(dq_out, row, g, dot_nn(kk.T, dscores) * SCALE)
            return 0

        lax.fori_loop(0, GROUPS, local, 0)

        def finish(g, _):
            far(2, g).wait_recv()
            dv_out[:, columns(g)] = (dv_sum[g] + dkv_far[2 * g].astype(F32)).astype(BF16)
            far(3, g).wait_recv()
            dk_out[:, columns(g)] = (dk_sum[g] * SCALE + dkv_far[2 * g + 1].astype(F32)).astype(BF16)
            return 0

        @pl.when(core == 0)
        def _():
            bias_lent[...] = mask_bias(lengths, seq, ROWS, 0, ROWS + HALF)
            for i in range(4):
                lend(i).wait_recv()
            kk = jnp.concatenate([k_own[:, columns(last)], lent[0]], axis=0)
            vv = jnp.concatenate([v_own[:, columns(last)], lent[1]], axis=0)
            qq = stacked(lent_wide.at[0], 0, 0)
            gg = stacked(lent_wide.at[1], 0, 0)
            probs = probabilities(kk, qq, bias_lent[...])
            rounded = probs.astype(BF16)
            dscores = score_gradient(probs, vv, gg)
            dv = dot_nn(rounded, gg)
            dk = dot_nn(dscores, qq) * SCALE
            dv_out[:, columns(last)] = (dv_sum[last] + dv[0:ROWS]).astype(BF16)
            dk_out[:, columns(last)] = (dk_sum[last] * SCALE + dk[0:ROWS]).astype(BF16)
            given[0] = dk[ROWS:].astype(BF16)
            given[1] = dv[ROWS:].astype(BF16)
            put_heads(given_wide.at[0], 0, 0, dot_nn(vv.T, rounded))
            put_heads(given_wide.at[1], 0, 0, dot_nn(kk.T, dscores) * SCALE)
            wait_sent(0, 2)
            wait_sent(1, 2 * GROUPS - 4)
            for i in range(4):
                give_back(i).start()
            lax.fori_loop(0, last, finish, 0)
            wait_sent(0, 6)

        @pl.when(core == 1)
        def _():
            lax.fori_loop(0, last, finish, 0)
            wait_sent(1, 2 * GROUPS - 2)
            finish(last, 0)

    @pl.when(head == 1)
    def _():
        load(4).start()
        load(2).start()
        load(3).start()
        pl.semaphore_wait(barrier, 1)

        @pl.when(core == 0)
        def _():
            for i in range(4):
                lend(i).start()

        load(4).wait()
        bias_a[...] = mask_bias(lengths, seq, ROWS, 0, ROWS + HALF)
        bias_b[...] = mask_bias(lengths, seq, ROWS + HALF, ROWS + HALF, HALF)
        for i in range(4):
            load(i).wait()

        def work_near(g):
            kk = k_own[HALF:ROWS, columns(g)]
            vv = v_own[HALF:ROWS, columns(g)]
            qq = stacked(q_own, HALF, g)
            gg = stacked(g_own, HALF, g)
            probs = probabilities(kk, qq, bias_b[...])
            rounded = probs.astype(BF16)
            dscores = score_gradient(probs, vv, gg)
            dv_out[HALF:ROWS, columns(g)] = dot_nn(rounded, gg).astype(BF16)
            dk_out[HALF:ROWS, columns(g)] = (dot_nn(dscores, qq) * SCALE).astype(BF16)
            put_heads(o_out, HALF, g, dot_nn(vv.T, rounded))
            put_heads(dq_out, HALF, g, dot_nn(kk.T, dscores) * SCALE)

        def work(g, _):
            work_near(g)
            k_near = k_own[0:HALF, columns(g)]
            v_near = v_own[0:HALF, columns(g)]
            qq = stacked(q_own, 0, g)
            gg = stacked(g_own, 0, g)
            near_logits = logits(k_near, qq, bias_a[ROWS:])
            near_top = jnp.max(near_logits, axis=0, keepdims=True)
            near_dprobs = dot_nt(v_near, gg)

            far(0, g).wait_recv()
            k_there = kv_far[2 * g]
            far_logits = logits(k_there, qq, bias_a[0:ROWS])
            top = jnp.maximum(near_top, jnp.max(far_logits, axis=0, keepdims=True))
            probs_far = jnp.exp2(far_logits - top)
            probs_near = jnp.exp2(near_logits - top)
            total = jnp.sum(probs_far, axis=0, keepdims=True)
            total += jnp.sum(probs_near, axis=0, keepdims=True)
            probs_far *= 1.0 / total
            probs_near *= 1.0 / total
            rounded_far = probs_far.astype(BF16)
            rounded_near = probs_near.astype(BF16)
            dkv_send[2 * g] = dot_nn(rounded_far, gg).astype(BF16)
            far(2, g).start()
            near_sum = jnp.sum(probs_near * near_dprobs, axis=0, keepdims=True)

            far(1, g).wait_recv()
            v_there = kv_far[2 * g + 1]
            dprobs = dot_nt(v_there, gg)
            delta = near_sum + jnp.sum(probs_far * dprobs, axis=0, keepdims=True)
            dscores_far = (probs_far * (dprobs - delta)).astype(BF16)
            dkv_send[2 * g + 1] = (dot_nn(dscores_far, qq) * SCALE).astype(BF16)
            far(3, g).start()
            dscores_near = (probs_near * (near_dprobs - delta)).astype(BF16)
            dv_out[0:HALF, columns(g)] = dot_nn(rounded_near, gg).astype(BF16)
            dk_out[0:HALF, columns(g)] = (dot_nn(dscores_near, qq) * SCALE).astype(BF16)
            vv = jnp.concatenate([v_there, v_near], axis=0)
            kk = jnp.concatenate([k_there, k_near], axis=0)
            rounded = jnp.concatenate([rounded_far, rounded_near], axis=0)
            dscores = jnp.concatenate([dscores_far, dscores_near], axis=0)
            put_heads(o_out, 0, g, dot_nn(vv.T, rounded))
            put_heads(dq_out, 0, g, dot_nn(kk.T, dscores) * SCALE)
            return 0

        lax.fori_loop(0, groups, work, 0)

        @pl.when(core == 0)
        def _():
            work_near(last)
            wait_sent(0, 6)
            wait_sent(1, 2 * GROUPS - 2)
            for i in range(4):
                give_back(i).wait_recv()
            wide = slice(last * WIDE, GROUPS * WIDE)
            o_out[0:HALF, wide] = lent_wide[0]
            dq_out[0:HALF, wide] = lent_wide[1]
            dk_out[0:HALF, columns(last)] = lent[0]
            dv_out[0:HALF, columns(last)] = lent[1]

        @pl.when(core == 1)
        def _():
            wait_sent(1, 2 * GROUPS)


def store_kernel(*refs):
    count = len(refs) // 2
    copies = [
        pltpu.make_async_copy(refs[i], refs[count + i], refs[-1].at[i]) for i in range(count)
    ]
    for copy in copies:
        copy.start()
    for copy in copies:
        copy.wait()


def body(queries, keys, values, output_gradient, document_lengths):
    hbm = pl.BlockSpec(memory_space=pl.ANY)
    blocks = pltpu.VMEM((2 * GROUPS, ROWS, WIDTH), BF16)
    total = pltpu.VMEM((GROUPS, ROWS, WIDTH), F32)
    results = pl.pallas_call(
        kernel,
        out_shape=[pltpu.VMEM(x.shape, BF16) for x in (queries, queries, keys, values)],
        in_specs=[hbm] * 5,
        scratch_shapes=[
            pltpu.VMEM(queries.shape, BF16),
            pltpu.VMEM(keys.shape, BF16),
            pltpu.VMEM(values.shape, BF16),
            pltpu.VMEM(queries.shape, BF16),
            blocks, blocks, blocks, total, total,
            pltpu.VMEM((2, HALF, WIDE), BF16),
            pltpu.VMEM((2, HALF, WIDTH), BF16),
            pltpu.VMEM((2, HALF, WIDE), BF16),
            pltpu.VMEM((2, HALF, WIDTH), BF16),
            pltpu.VMEM((ROWS + HALF, HALF), F32),
            pltpu.VMEM((HALF, HALF), F32),
            pltpu.VMEM((ROWS + HALF, HALF), F32),
            pltpu.SMEM(document_lengths.shape[::-1], jnp.int32),
            pltpu.SemaphoreType.DMA((5,)),
            pltpu.SemaphoreType.DMA((2,)),
            pltpu.SemaphoreType.DMA((2 * GROUPS + 2,)),
        ],
        compiler_params=pltpu.CompilerParams(
            collective_id=0, has_side_effects=True, vmem_limit_bytes=54 << 20
        ),
        name="packed_attention",
    )(document_lengths.T, queries, keys, values, output_gradient)
    return pl.pallas_call(
        store_kernel,
        out_shape=[jax.ShapeDtypeStruct(x.shape, BF16) for x in results],
        in_specs=[pl.BlockSpec(memory_space=pltpu.VMEM)] * len(results),
        out_specs=[hbm] * len(results),
        scratch_shapes=[pltpu.SemaphoreType.DMA((len(results),))],
        compiler_params=pltpu.CompilerParams(vmem_limit_bytes=16 << 20),
        name="store_results",
    )(*[pltpu.with_memory_space_constraint(x, pltpu.VMEM) for x in results])


def solution(mesh):
    rows = P(("seq", "head"), None)
    return jax.shard_map(
        body,
        mesh=mesh,
        in_specs=(rows, rows, rows, rows, P()),
        out_specs=(rows, rows, rows, rows),
        check_vma=False,
    )
```

```python
import functools
import math

import jax
import jax.numpy as jnp
from jax import lax
from jax.experimental import pallas as pl
from jax.experimental.pallas import tpu as pltpu
from jax.sharding import PartitionSpec as P

QUERY_HEADS = 40
GROUPS = 8
RATIO = QUERY_HEADS // GROUPS
WIDTH = 128
WIDE = RATIO * WIDTH
ROWS = 256
HALF = 128
DOCS = 16
NEG = -1e30
SCALE = 1.0 / math.sqrt(WIDTH)
TO_EXP2 = SCALE * math.log2(math.e)
MESH = pl.DeviceIdType.MESH
F32 = jnp.float32
BF16 = jnp.bfloat16


def dot_nt(a, b):
    return lax.dot_general(a, b, (((1,), (1,)), ((), ())), preferred_element_type=F32)


def dot_nn(a, b):
    return jnp.dot(a, b, preferred_element_type=F32)


def stacked(ref, row, group):
    return jnp.concatenate(
        [
            ref[pl.ds(row, HALF), columns(group * RATIO + h)]
            for h in range(RATIO)
        ],
        axis=0,
    )


def columns(group):
    if isinstance(group, int):
        return slice(group * WIDTH, (group + 1) * WIDTH)
    return pl.ds(pl.multiple_of(group * WIDTH, WIDTH), WIDTH)


def logits(keys, queries, bias):
    return dot_nt(keys, queries) * TO_EXP2 + jnp.concatenate([bias] * RATIO, axis=1)


def probabilities(keys, queries, bias):
    scaled = logits(keys, queries, bias)
    weights = jnp.exp2(scaled - jnp.max(scaled, axis=0, keepdims=True))
    return weights * (1.0 / jnp.sum(weights, axis=0, keepdims=True))


def score_gradient(probs, values, grads):
    dprobs = dot_nt(values, grads)
    delta = jnp.sum(probs * dprobs, axis=0, keepdims=True)
    return (probs * (dprobs - delta)).astype(BF16)


def put_heads(ref, row, group, transposed):
    for h in range(RATIO):
        block = transposed[:, h * WIDTH : (h + 1) * WIDTH].T
        ref[pl.ds(row, HALF), columns(group * RATIO + h)] = block.astype(BF16)


def mask_bias(lengths, block, first_query, first_key, keys):
    query = first_query + lax.broadcasted_iota(jnp.int32, (1, HALF), 1)
    start = jnp.int32(0)
    doc_start = jnp.zeros((1, HALF), jnp.int32)
    for d in range(DOCS):
        doc_start = jnp.where(query >= start, start, doc_start)
        start = start + lengths[d, block]
    key = first_key + lax.broadcasted_iota(jnp.int32, (keys, HALF), 0)
    return jnp.where((key >= doc_start) & (key <= query), 0.0, NEG).astype(F32)


def kernel(
    lengths_hbm, q_hbm, k_hbm, v_hbm, g_hbm,
    o_out, dq_out, dk_out, dv_out,
    q_own, k_own, v_own, g_own,
    kv_far, dkv_send, dkv_far, dk_sum, dv_sum,
    lent_wide, lent, given_wide, given,
    bias_a, bias_b, bias_lent, lengths, load_sem, send_sem, recv_sem,
):
    seq = lax.axis_index("seq")
    head = lax.axis_index("head")
    core = lax.rem(seq, 2)
    last = GROUPS - 1
    groups = jnp.where(core == 1, last, GROUPS)
    partner = (seq, 1 - head)
    barrier = pltpu.get_barrier_semaphore()
    pl.semaphore_signal(barrier, inc=1, device_id=partner, device_id_type=MESH)

    def load(i):
        src, dst = (
            (k_hbm, k_own), (v_hbm, v_own), (q_hbm, q_own), (g_hbm, g_own), (lengths_hbm, lengths)
        )[i]
        return pltpu.make_async_copy(src, dst, load_sem.at[i])

    def send(src, dst, sent, landed):
        return pltpu.make_async_remote_copy(
            src_ref=src,
            dst_ref=dst,
            send_sem=send_sem.at[sent],
            recv_sem=recv_sem.at[landed],
            device_id=partner,
            device_id_type=MESH,
        )

    def far(i, g, sent=1):
        at = 2 * g + i % 2
        if i < 2:
            return send((k_own, v_own)[i].at[:, columns(g)], kv_far.at[at], sent, at)
        return send(dkv_send.at[at], dkv_far.at[at], sent, at)

    def lend(i):
        rows, wide, narrow = slice(0, HALF), slice(last * WIDE, GROUPS * WIDE), columns(last)
        src = (q_hbm.at[rows, wide], g_hbm.at[rows, wide], k_hbm.at[rows, narrow], v_hbm.at[rows, narrow])
        dst = (lent_wide if i < 2 else lent).at[i % 2]
        return send(src[i], dst, 0, 2 * GROUPS - 2 + i)

    def give_back(i):
        src, dst = (given_wide, lent_wide) if i < 2 else (given, lent)
        return send(src.at[i % 2], dst.at[i % 2], 0, 2 * GROUPS - 2 + i)

    def wait_sent(sent, blocks):
        every = kv_far.at[0:blocks]
        send(every, every, sent, 0).wait_send()

    load(0).start()
    load(1).start()

    @pl.when(head == 0)
    def _():
        pl.semaphore_wait(barrier, 1)
        load(0).wait()
        far(0, 0, 0).start()
        load(1).wait()
        far(1, 0, 0).start()

        @pl.when(core == 1)
        def _():
            wait_sent(0, 2)

        def send_group(g, _):
            far(0, g).start()
            far(1, g).start()
            return 0

        lax.fori_loop(1, 2, send_group, 0)

        @pl.when(core == 1)
        def _():
            wait_sent(1, 2)

        lax.fori_loop(2, groups, send_group, 0)
        load(4).start()
        load(2).start()
        load(3).start()
        load(4).wait()
        bias_a[0:ROWS] = mask_bias(lengths, seq, HALF, 0, ROWS)
        bias_b[...] = mask_bias(lengths, seq, 0, 0, HALF)
        load(2).wait()
        load(3).wait()

        def local(g, _):
            for row, keys, bias in ((HALF, ROWS, bias_a), (0, HALF, bias_b)):
                kk = k_own[0:keys, columns(g)]
                vv = v_own[0:keys, columns(g)]
                qq = stacked(q_own, row, g)
                gg = stacked(g_own, row, g)
                probs = probabilities(kk, qq, bias[0:keys])
                rounded = probs.astype(BF16)
                dscores = score_gradient(probs, vv, gg)
                dv = dot_nn(rounded, gg)
                dk = dot_nn(dscores, qq)
                if row:
                    dv_sum[g] = dv
                    dk_sum[g] = dk
                else:
                    dv_sum[g, 0:HALF] += dv
                    dk_sum[g, 0:HALF] += dk
                put_heads(o_out, row, g, dot_nn(vv.T, rounded))
                put_heads(dq_out, row, g, dot_nn(kk.T, dscores) * SCALE)
            return 0

        lax.fori_loop(0, GROUPS, local, 0)

        def finish(g, _):
            far(2, g).wait_recv()
            dv_out[:, columns(g)] = (dv_sum[g] + dkv_far[2 * g].astype(F32)).astype(BF16)
            far(3, g).wait_recv()
            dk_out[:, columns(g)] = (dk_sum[g] * SCALE + dkv_far[2 * g + 1].astype(F32)).astype(BF16)
            return 0

        @pl.when(core == 1)
        def _():
            bias_lent[...] = mask_bias(lengths, seq, ROWS, 0, ROWS + HALF)
            for i in range(4):
                lend(i).wait_recv()
            kk = jnp.concatenate([k_own[:, columns(last)], lent[0]], axis=0)
            vv = jnp.concatenate([v_own[:, columns(last)], lent[1]], axis=0)
            qq = stacked(lent_wide.at[0], 0, 0)
            gg = stacked(lent_wide.at[1], 0, 0)
            probs = probabilities(kk, qq, bias_lent[...])
            rounded = probs.astype(BF16)
            dscores = score_gradient(probs, vv, gg)
            dv = dot_nn(rounded, gg)
            dk = dot_nn(dscores, qq) * SCALE
            dv_out[:, columns(last)] = (dv_sum[last] + dv[0:ROWS]).astype(BF16)
            dk_out[:, columns(last)] = (dk_sum[last] * SCALE + dk[0:ROWS]).astype(BF16)
            given[0] = dk[ROWS:].astype(BF16)
            given[1] = dv[ROWS:].astype(BF16)
            put_heads(given_wide.at[0], 0, 0, dot_nn(vv.T, rounded))
            put_heads(given_wide.at[1], 0, 0, dot_nn(kk.T, dscores) * SCALE)
            wait_sent(1, 2 * GROUPS - 6)
            lax.fori_loop(0, 0, finish, 0)
            for i in range(4):
                give_back(i).start()
            lax.fori_loop(0, last, finish, 0)
            wait_sent(0, 6)

        @pl.when(core == 0)
        def _():
            lax.fori_loop(0, last, finish, 0)
            wait_sent(0, 2)
            wait_sent(1, 2 * GROUPS - 2)
            finish(last, 0)

    @pl.when(head == 1)
    def _():
        load(4).start()
        load(2).start()
        load(3).start()
        pl.semaphore_wait(barrier, 1)

        @pl.when(core == 1)
        def _():
            for i in range(4):
                lend(i).start()

        load(4).wait()
        bias_a[...] = mask_bias(lengths, seq, ROWS, 0, ROWS + HALF)
        bias_b[...] = mask_bias(lengths, seq, ROWS + HALF, ROWS + HALF, HALF)
        for i in range(4):
            load(i).wait()

        def work_near(g):
            kk = k_own[HALF:ROWS, columns(g)]
            vv = v_own[HALF:ROWS, columns(g)]
            qq = stacked(q_own, HALF, g)
            gg = stacked(g_own, HALF, g)
            probs = probabilities(kk, qq, bias_b[...])
            rounded = probs.astype(BF16)
            dscores = score_gradient(probs, vv, gg)
            dv_out[HALF:ROWS, columns(g)] = dot_nn(rounded, gg).astype(BF16)
            dk_out[HALF:ROWS, columns(g)] = (dot_nn(dscores, qq) * SCALE).astype(BF16)
            put_heads(o_out, HALF, g, dot_nn(vv.T, rounded))
            put_heads(dq_out, HALF, g, dot_nn(kk.T, dscores) * SCALE)

        def work(g, _):
            work_near(g)
            k_near = k_own[0:HALF, columns(g)]
            v_near = v_own[0:HALF, columns(g)]
            qq = stacked(q_own, 0, g)
            gg = stacked(g_own, 0, g)
            near_logits = logits(k_near, qq, bias_a[ROWS:])
            near_top = jnp.max(near_logits, axis=0, keepdims=True)
            near_dprobs = dot_nt(v_near, gg)

            far(0, g).wait_recv()
            k_there = kv_far[2 * g]
            far_logits = logits(k_there, qq, bias_a[0:ROWS])
            top = jnp.maximum(near_top, jnp.max(far_logits, axis=0, keepdims=True))
            probs_far = jnp.exp2(far_logits - top)
            probs_near = jnp.exp2(near_logits - top)
            total = jnp.sum(probs_far, axis=0, keepdims=True)
            total += jnp.sum(probs_near, axis=0, keepdims=True)
            probs_far *= 1.0 / total
            probs_near *= 1.0 / total
            rounded_far = probs_far.astype(BF16)
            rounded_near = probs_near.astype(BF16)
            dkv_send[2 * g] = dot_nn(rounded_far, gg).astype(BF16)
            far(2, g).start()
            near_sum = jnp.sum(probs_near * near_dprobs, axis=0, keepdims=True)

            far(1, g).wait_recv()
            v_there = kv_far[2 * g + 1]
            dprobs = dot_nt(v_there, gg)
            delta = near_sum + jnp.sum(probs_far * dprobs, axis=0, keepdims=True)
            dscores_far = (probs_far * (dprobs - delta)).astype(BF16)
            dkv_send[2 * g + 1] = (dot_nn(dscores_far, qq) * SCALE).astype(BF16)
            far(3, g).start()
            dscores_near = (probs_near * (near_dprobs - delta)).astype(BF16)
            dv_out[0:HALF, columns(g)] = dot_nn(rounded_near, gg).astype(BF16)
            dk_out[0:HALF, columns(g)] = (dot_nn(dscores_near, qq) * SCALE).astype(BF16)
            vv = jnp.concatenate([v_there, v_near], axis=0)
            kk = jnp.concatenate([k_there, k_near], axis=0)
            rounded = jnp.concatenate([rounded_far, rounded_near], axis=0)
            dscores = jnp.concatenate([dscores_far, dscores_near], axis=0)
            put_heads(o_out, 0, g, dot_nn(vv.T, rounded))
            put_heads(dq_out, 0, g, dot_nn(kk.T, dscores) * SCALE)
            return 0

        lax.fori_loop(0, groups, work, 0)

        @pl.when(core == 1)
        def _():
            work_near(last)
            wait_sent(0, 6)
            wait_sent(1, 2 * GROUPS - 2)
            for i in range(4):
                give_back(i).wait_recv()
            wide = slice(last * WIDE, GROUPS * WIDE)
            o_out[0:HALF, wide] = lent_wide[0]
            dq_out[0:HALF, wide] = lent_wide[1]
            dk_out[0:HALF, columns(last)] = lent[0]
            dv_out[0:HALF, columns(last)] = lent[1]

        @pl.when(core == 0)
        def _():
            wait_sent(1, 2 * GROUPS)


def store_kernel(*refs):
    count = len(refs) // 2
    copies = [
        pltpu.make_async_copy(refs[i], refs[count + i], refs[-1].at[i]) for i in range(count)
    ]
    for copy in copies:
        copy.start()
    for copy in copies:
        copy.wait()


def body(queries, keys, values, output_gradient, document_lengths):
    hbm = pl.BlockSpec(memory_space=pl.ANY)
    blocks = pltpu.VMEM((2 * GROUPS, ROWS, WIDTH), BF16)
    total = pltpu.VMEM((GROUPS, ROWS, WIDTH), F32)
    results = pl.pallas_call(
        kernel,
        out_shape=[pltpu.VMEM(x.shape, BF16) for x in (queries, queries, keys, values)],
        in_specs=[hbm] * 5,
        scratch_shapes=[
            pltpu.VMEM(queries.shape, BF16),
            pltpu.VMEM(keys.shape, BF16),
            pltpu.VMEM(values.shape, BF16),
            pltpu.VMEM(queries.shape, BF16),
            blocks, blocks, blocks, total, total,
            pltpu.VMEM((2, HALF, WIDE), BF16),
            pltpu.VMEM((2, HALF, WIDTH), BF16),
            pltpu.VMEM((2, HALF, WIDE), BF16),
            pltpu.VMEM((2, HALF, WIDTH), BF16),
            pltpu.VMEM((ROWS + HALF, HALF), F32),
            pltpu.VMEM((HALF, HALF), F32),
            pltpu.VMEM((ROWS + HALF, HALF), F32),
            pltpu.SMEM(document_lengths.shape[::-1], jnp.int32),
            pltpu.SemaphoreType.DMA((5,)),
            pltpu.SemaphoreType.DMA((2,)),
            pltpu.SemaphoreType.DMA((2 * GROUPS + 2,)),
        ],
        compiler_params=pltpu.CompilerParams(
            collective_id=0, has_side_effects=True, vmem_limit_bytes=54 << 20
        ),
        name="packed_attention",
    )(document_lengths.T, queries, keys, values, output_gradient)
    return pl.pallas_call(
        store_kernel,
        out_shape=[jax.ShapeDtypeStruct(x.shape, BF16) for x in results],
        in_specs=[pl.BlockSpec(memory_space=pltpu.VMEM)] * len(results),
        out_specs=[hbm] * len(results),
        scratch_shapes=[pltpu.SemaphoreType.DMA((len(results),))],
        compiler_params=pltpu.CompilerParams(vmem_limit_bytes=16 << 20),
        name="store_results",
    )(*[pltpu.with_memory_space_constraint(x, pltpu.VMEM) for x in results])


def solution(mesh):
    rows = P(("seq", "head"), None)
    return jax.shard_map(
        body,
        mesh=mesh,
        in_specs=(rows, rows, rows, rows, P()),
        out_specs=(rows, rows, rows, rows),
        check_vma=False,
    )
```

```python
import functools
import math

import jax
import jax.numpy as jnp
from jax import lax
from jax.experimental import pallas as pl
from jax.experimental.pallas import tpu as pltpu
from jax.sharding import PartitionSpec as P

QUERY_HEADS = 40
GROUPS = 8
RATIO = QUERY_HEADS // GROUPS
WIDTH = 128
WIDE = RATIO * WIDTH
ROWS = 256
HALF = 128
DOCS = 16
NEG = -1e30
SCALE = 1.0 / math.sqrt(WIDTH)
TO_EXP2 = SCALE * math.log2(math.e)
MESH = pl.DeviceIdType.MESH
F32 = jnp.float32
BF16 = jnp.bfloat16


def dot_nt(a, b):
    return lax.dot_general(a, b, (((1,), (1,)), ((), ())), preferred_element_type=F32)


def dot_tn(a, b):
    return lax.dot_general(a, b, (((0,), (0,)), ((), ())), preferred_element_type=F32)


def dot_nn(a, b):
    return jnp.dot(a, b, preferred_element_type=F32)


def stacked(ref, row, group):
    return jnp.concatenate(
        [
            ref[pl.ds(row, HALF), columns(group * RATIO + h)]
            for h in range(RATIO)
        ],
        axis=0,
    )


def columns(group):
    if isinstance(group, int):
        return slice(group * WIDTH, (group + 1) * WIDTH)
    return pl.ds(pl.multiple_of(group * WIDTH, WIDTH), WIDTH)


def logits(keys, queries, bias):
    return dot_nt(keys, queries) * TO_EXP2 + jnp.concatenate([bias] * RATIO, axis=1)


def probabilities(keys, queries, bias):
    scaled = logits(keys, queries, bias)
    weights = jnp.exp2(scaled - jnp.max(scaled, axis=0, keepdims=True))
    return weights * (1.0 / jnp.sum(weights, axis=0, keepdims=True))


def score_gradient(probs, values, grads):
    dprobs = dot_nt(values, grads)
    delta = jnp.sum(probs * dprobs, axis=0, keepdims=True)
    return (probs * (dprobs - delta)).astype(BF16)


def put_heads(ref, row, group, transposed):
    for h in range(RATIO):
        block = transposed[h * WIDTH : (h + 1) * WIDTH]
        ref[pl.ds(row, HALF), columns(group * RATIO + h)] = block.astype(BF16)


def mask_bias(lengths, block, first_query, first_key, keys):
    query = first_query + lax.broadcasted_iota(jnp.int32, (1, HALF), 1)
    start = jnp.int32(0)
    doc_start = jnp.zeros((1, HALF), jnp.int32)
    for d in range(DOCS):
        doc_start = jnp.where(query >= start, start, doc_start)
        start = start + lengths[d, block]
    key = first_key + lax.broadcasted_iota(jnp.int32, (keys, HALF), 0)
    return jnp.where((key >= doc_start) & (key <= query), 0.0, NEG).astype(F32)


def kernel(
    lengths_hbm, q_hbm, k_hbm, v_hbm, g_hbm,
    o_out, dq_out, dk_out, dv_out,
    q_own, k_own, v_own, g_own,
    kv_far, dkv_send, dkv_far, dk_sum, dv_sum,
    lent_wide, lent, given_wide, given,
    bias_a, bias_b, bias_lent, lengths, load_sem, send_sem, recv_sem,
):
    seq = lax.axis_index("seq")
    head = lax.axis_index("head")
    core = lax.rem(seq, 2)
    last = GROUPS - 1
    groups = jnp.where(core == 1, last, GROUPS)
    partner = (seq, 1 - head)
    barrier = pltpu.get_barrier_semaphore()
    pl.semaphore_signal(barrier, inc=1, device_id=partner, device_id_type=MESH)

    def load(i):
        src, dst = (
            (k_hbm, k_own), (v_hbm, v_own), (q_hbm, q_own), (g_hbm, g_own), (lengths_hbm, lengths)
        )[i]
        return pltpu.make_async_copy(src, dst, load_sem.at[i])

    def send(src, dst, sent, landed):
        return pltpu.make_async_remote_copy(
            src_ref=src,
            dst_ref=dst,
            send_sem=send_sem.at[sent],
            recv_sem=recv_sem.at[landed],
            device_id=partner,
            device_id_type=MESH,
        )

    def far(i, g, sent=1):
        at = 2 * g + i % 2
        if i < 2:
            return send((k_own, v_own)[i].at[:, columns(g)], kv_far.at[at], sent, at)
        return send(dkv_send.at[at], dkv_far.at[at], sent, at)

    def lend(i):
        rows, wide, narrow = slice(0, HALF), slice(last * WIDE, GROUPS * WIDE), columns(last)
        src = (q_hbm.at[rows, wide], g_hbm.at[rows, wide], k_hbm.at[rows, narrow], v_hbm.at[rows, narrow])
        dst = (lent_wide if i < 2 else lent).at[i % 2]
        return send(src[i], dst, 0, 2 * GROUPS - 2 + i // 2)

    def give_back(i):
        src, dst = (given_wide, lent_wide) if i < 2 else (given, lent)
        return send(src.at[i % 2], dst.at[i % 2], 0, 2 * GROUPS - 2 + i // 2)

    def wait_lent():
        send(lent_wide, lent_wide, 0, 2 * GROUPS - 2).wait_recv()
        send(lent, lent, 0, 2 * GROUPS - 1).wait_recv()

    def wait_sent(sent, blocks):
        every = kv_far.at[0:blocks]
        send(every, every, sent, 0).wait_send()

    load(0).start()
    load(1).start()

    @pl.when(head == 0)
    def _():
        pl.semaphore_wait(barrier, 1)
        load(0).wait()
        far(0, 0, 0).start()
        load(1).wait()
        far(1, 0, 0).start()

        @pl.when(core == 1)
        def _():
            wait_sent(0, 2)

        def send_group(g, _):
            far(0, g).start()
            far(1, g).start()
            return 0

        lax.fori_loop(1, 2, send_group, 0)

        @pl.when(core == 1)
        def _():
            wait_sent(1, 2)

        lax.fori_loop(2, groups, send_group, 0)
        load(4).start()
        load(2).start()
        load(3).start()
        load(4).wait()
        bias_a[0:ROWS] = mask_bias(lengths, seq, HALF, 0, ROWS)
        bias_b[...] = mask_bias(lengths, seq, 0, 0, HALF)
        load(2).wait()
        load(3).wait()

        def local(g, _):
            for row, keys, bias in ((HALF, ROWS, bias_a), (0, HALF, bias_b)):
                kk = k_own[0:keys, columns(g)]
                vv = v_own[0:keys, columns(g)]
                qq = stacked(q_own, row, g)
                gg = stacked(g_own, row, g)
                probs = probabilities(kk, qq, bias[0:keys])
                rounded = probs.astype(BF16)
                dscores = score_gradient(probs, vv, gg)
                dv = dot_nn(rounded, gg)
                dk = dot_nn(dscores, qq)
                if row:
                    dv_sum[g] = dv
                    dk_sum[g] = dk
                else:
                    dv_sum[g, 0:HALF] += dv
                    dk_sum[g, 0:HALF] += dk
                put_heads(o_out, row, g, dot_tn(rounded, vv))
                put_heads(dq_out, row, g, dot_tn(dscores, kk) * SCALE)
            return 0

        lax.fori_loop(0, GROUPS, local, 0)

        def finish(g, _):
            far(2, g).wait_recv()
            dv_out[:, columns(g)] = (dv_sum[g] + dkv_far[2 * g].astype(F32)).astype(BF16)
            far(3, g).wait_recv()
            dk_out[:, columns(g)] = (dk_sum[g] * SCALE + dkv_far[2 * g + 1].astype(F32)).astype(BF16)
            return 0

        @pl.when(core == 1)
        def _():
            bias_lent[...] = mask_bias(lengths, seq, ROWS, 0, ROWS + HALF)
            wait_lent()
            kk = jnp.concatenate([k_own[:, columns(last)], lent[0]], axis=0)
            vv = jnp.concatenate([v_own[:, columns(last)], lent[1]], axis=0)
            qq = stacked(lent_wide.at[0], 0, 0)
            gg = stacked(lent_wide.at[1], 0, 0)
            probs = probabilities(kk, qq, bias_lent[...])
            rounded = probs.astype(BF16)
            dscores = score_gradient(probs, vv, gg)
            dv = dot_nn(rounded, gg)
            dk = dot_nn(dscores, qq) * SCALE
            dv_out[:, columns(last)] = (dv_sum[last] + dv[0:ROWS]).astype(BF16)
            dk_out[:, columns(last)] = (dk_sum[last] * SCALE + dk[0:ROWS]).astype(BF16)
            given[0] = dk[ROWS:].astype(BF16)
            given[1] = dv[ROWS:].astype(BF16)
            put_heads(given_wide.at[0], 0, 0, dot_tn(rounded, vv))
            put_heads(given_wide.at[1], 0, 0, dot_tn(dscores, kk) * SCALE)
            wait_sent(1, 2 * GROUPS - 6)
            lax.fori_loop(0, 0, finish, 0)
            for i in range(4):
                give_back(i).start()
            lax.fori_loop(0, last, finish, 0)
            wait_sent(0, 6)

        @pl.when(core == 0)
        def _():
            lax.fori_loop(0, last, finish, 0)
            wait_sent(0, 2)
            wait_sent(1, 2 * GROUPS - 2)
            finish(last, 0)

    @pl.when(head == 1)
    def _():
        load(4).start()
        load(2).start()
        load(3).start()
        pl.semaphore_wait(barrier, 1)

        @pl.when(core == 1)
        def _():
            for i in range(4):
                lend(i).start()

        load(4).wait()
        bias_a[...] = mask_bias(lengths, seq, ROWS, 0, ROWS + HALF)
        bias_b[...] = mask_bias(lengths, seq, ROWS + HALF, ROWS + HALF, HALF)
        for i in range(4):
            load(i).wait()

        def work_near(g):
            kk = k_own[HALF:ROWS, columns(g)]
            vv = v_own[HALF:ROWS, columns(g)]
            qq = stacked(q_own, HALF, g)
            gg = stacked(g_own, HALF, g)
            probs = probabilities(kk, qq, bias_b[...])
            rounded = probs.astype(BF16)
            dscores = score_gradient(probs, vv, gg)
            dv_out[HALF:ROWS, columns(g)] = dot_nn(rounded, gg).astype(BF16)
            dk_out[HALF:ROWS, columns(g)] = (dot_nn(dscores, qq) * SCALE).astype(BF16)
            put_heads(o_out, HALF, g, dot_tn(rounded, vv))
            put_heads(dq_out, HALF, g, dot_tn(dscores, kk) * SCALE)

        def work(g, _):
            work_near(g)
            k_near = k_own[0:HALF, columns(g)]
            v_near = v_own[0:HALF, columns(g)]
            qq = stacked(q_own, 0, g)
            gg = stacked(g_own, 0, g)
            near_logits = logits(k_near, qq, bias_a[ROWS:])
            near_top = jnp.max(near_logits, axis=0, keepdims=True)
            near_dprobs = dot_nt(v_near, gg)

            far(0, g).wait_recv()
            k_there = kv_far[2 * g]
            far_logits = logits(k_there, qq, bias_a[0:ROWS])
            top = jnp.maximum(near_top, jnp.max(far_logits, axis=0, keepdims=True))
            probs_far = jnp.exp2(far_logits - top)
            probs_near = jnp.exp2(near_logits - top)
            total = jnp.sum(probs_far, axis=0, keepdims=True)
            total += jnp.sum(probs_near, axis=0, keepdims=True)
            probs_far *= 1.0 / total
            probs_near *= 1.0 / total
            rounded_far = probs_far.astype(BF16)
            rounded_near = probs_near.astype(BF16)
            dkv_send[2 * g] = dot_nn(rounded_far, gg).astype(BF16)
            far(2, g).start()
            near_sum = jnp.sum(probs_near * near_dprobs, axis=0, keepdims=True)

            far(1, g).wait_recv()
            v_there = kv_far[2 * g + 1]
            dprobs = dot_nt(v_there, gg)
            delta = near_sum + jnp.sum(probs_far * dprobs, axis=0, keepdims=True)
            dscores_far = (probs_far * (dprobs - delta)).astype(BF16)
            dkv_send[2 * g + 1] = (dot_nn(dscores_far, qq) * SCALE).astype(BF16)
            far(3, g).start()
            dscores_near = (probs_near * (near_dprobs - delta)).astype(BF16)
            dv_out[0:HALF, columns(g)] = dot_nn(rounded_near, gg).astype(BF16)
            dk_out[0:HALF, columns(g)] = (dot_nn(dscores_near, qq) * SCALE).astype(BF16)
            vv = jnp.concatenate([v_there, v_near], axis=0)
            kk = jnp.concatenate([k_there, k_near], axis=0)
            rounded = jnp.concatenate([rounded_far, rounded_near], axis=0)
            dscores = jnp.concatenate([dscores_far, dscores_near], axis=0)
            put_heads(o_out, 0, g, dot_tn(rounded, vv))
            put_heads(dq_out, 0, g, dot_tn(dscores, kk) * SCALE)
            return 0

        lax.fori_loop(0, groups, work, 0)

        @pl.when(core == 1)
        def _():
            work_near(last)
            wait_sent(0, 6)
            wait_sent(1, 2 * GROUPS - 2)
            wait_lent()
            wide = slice(last * WIDE, GROUPS * WIDE)
            o_out[0:HALF, wide] = lent_wide[0]
            dq_out[0:HALF, wide] = lent_wide[1]
            dk_out[0:HALF, columns(last)] = lent[0]
            dv_out[0:HALF, columns(last)] = lent[1]

        @pl.when(core == 0)
        def _():
            wait_sent(1, 2 * GROUPS)


def store_kernel(*refs):
    count = len(refs) // 2
    copies = [
        pltpu.make_async_copy(refs[i], refs[count + i], refs[-1].at[i]) for i in range(count)
    ]
    for copy in copies:
        copy.start()
    for copy in copies:
        copy.wait()


def body(queries, keys, values, output_gradient, document_lengths):
    hbm = pl.BlockSpec(memory_space=pl.ANY)
    blocks = pltpu.VMEM((2 * GROUPS, ROWS, WIDTH), BF16)
    total = pltpu.VMEM((GROUPS, ROWS, WIDTH), F32)
    results = pl.pallas_call(
        kernel,
        out_shape=[pltpu.VMEM(x.shape, BF16) for x in (queries, queries, keys, values)],
        in_specs=[hbm] * 5,
        scratch_shapes=[
            pltpu.VMEM(queries.shape, BF16),
            pltpu.VMEM(keys.shape, BF16),
            pltpu.VMEM(values.shape, BF16),
            pltpu.VMEM(queries.shape, BF16),
            blocks, blocks, blocks, total, total,
            pltpu.VMEM((2, HALF, WIDE), BF16),
            pltpu.VMEM((2, HALF, WIDTH), BF16),
            pltpu.VMEM((2, HALF, WIDE), BF16),
            pltpu.VMEM((2, HALF, WIDTH), BF16),
            pltpu.VMEM((ROWS + HALF, HALF), F32),
            pltpu.VMEM((HALF, HALF), F32),
            pltpu.VMEM((ROWS + HALF, HALF), F32),
            pltpu.SMEM(document_lengths.shape[::-1], jnp.int32),
            pltpu.SemaphoreType.DMA((5,)),
            pltpu.SemaphoreType.DMA((2,)),
            pltpu.SemaphoreType.DMA((2 * GROUPS,)),
        ],
        compiler_params=pltpu.CompilerParams(
            collective_id=0, has_side_effects=True, vmem_limit_bytes=54 << 20
        ),
        name="packed_attention",
    )(document_lengths.T, queries, keys, values, output_gradient)
    return pl.pallas_call(
        store_kernel,
        out_shape=[jax.ShapeDtypeStruct(x.shape, BF16) for x in results],
        in_specs=[pl.BlockSpec(memory_space=pltpu.VMEM)] * len(results),
        out_specs=[hbm] * len(results),
        scratch_shapes=[pltpu.SemaphoreType.DMA((len(results),))],
        compiler_params=pltpu.CompilerParams(vmem_limit_bytes=16 << 20),
        name="store_results",
    )(*[pltpu.with_memory_space_constraint(x, pltpu.VMEM) for x in results])


def solution(mesh):
    rows = P(("seq", "head"), None)
    return jax.shard_map(
        body,
        mesh=mesh,
        in_specs=(rows, rows, rows, rows, P()),
        out_specs=(rows, rows, rows, rows),
        check_vma=False,
    )
```

```python
import functools
import math

import jax
import jax.numpy as jnp
from jax import lax
from jax.experimental import pallas as pl
from jax.experimental.pallas import tpu as pltpu
from jax.sharding import PartitionSpec as P

QUERY_HEADS = 40
GROUPS = 8
RATIO = QUERY_HEADS // GROUPS
WIDTH = 128
WIDE = RATIO * WIDTH
ROWS = 256
HALF = 128
DOCS = 16
NEG = -1e30
SCALE = 1.0 / math.sqrt(WIDTH)
TO_EXP2 = SCALE * math.log2(math.e)
MESH = pl.DeviceIdType.MESH
F32 = jnp.float32
BF16 = jnp.bfloat16


def dot_nt(a, b):
    return lax.dot_general(a, b, (((1,), (1,)), ((), ())), preferred_element_type=F32)


def dot_tn(a, b):
    return lax.dot_general(a, b, (((0,), (0,)), ((), ())), preferred_element_type=F32)


def dot_nn(a, b):
    return jnp.dot(a, b, preferred_element_type=F32)


def stacked(ref, row, group):
    return jnp.concatenate(
        [
            ref[pl.ds(row, HALF), columns(group * RATIO + h)]
            for h in range(RATIO)
        ],
        axis=0,
    )


def columns(group):
    if isinstance(group, int):
        return slice(group * WIDTH, (group + 1) * WIDTH)
    return pl.ds(pl.multiple_of(group * WIDTH, WIDTH), WIDTH)


def logits(keys, queries, bias):
    return dot_nt(keys, queries) * TO_EXP2 + jnp.concatenate([bias] * RATIO, axis=1)


def probabilities(keys, queries, bias):
    scaled = logits(keys, queries, bias)
    weights = jnp.exp2(scaled - jnp.max(scaled, axis=0, keepdims=True))
    return weights * (1.0 / jnp.sum(weights, axis=0, keepdims=True))


def score_gradient(probs, values, grads):
    dprobs = dot_nt(values, grads)
    delta = jnp.sum(probs * dprobs, axis=0, keepdims=True)
    return (probs * (dprobs - delta)).astype(BF16)


def put_heads(ref, row, group, transposed):
    for h in range(RATIO):
        block = transposed[h * WIDTH : (h + 1) * WIDTH]
        ref[pl.ds(row, HALF), columns(group * RATIO + h)] = block.astype(BF16)


def mask_bias(lengths, block, first_query, first_key, keys):
    query = first_query + lax.broadcasted_iota(jnp.int32, (1, HALF), 1)
    start = jnp.int32(0)
    doc_start = jnp.zeros((1, HALF), jnp.int32)
    for d in range(DOCS):
        doc_start = jnp.where(query >= start, start, doc_start)
        start = start + lengths[d, block]
    key = first_key + lax.broadcasted_iota(jnp.int32, (keys, HALF), 0)
    return jnp.where((key >= doc_start) & (key <= query), 0.0, NEG).astype(F32)


def kernel(
    lengths_hbm, q_hbm, k_hbm, v_hbm, g_hbm,
    o_out, dq_out, dk_out, dv_out,
    q_own, k_own, v_own, g_own,
    kv_far, dkv_send, dkv_far, dk_sum, dv_sum,
    lent_wide, lent, given_wide, given,
    bias_a, bias_b, bias_lent, lengths, load_sem, send_sem, recv_sem,
):
    seq = lax.axis_index("seq")
    head = lax.axis_index("head")
    core = lax.rem(seq, 2)
    last = GROUPS - 1
    groups = jnp.where(core == 1, last, GROUPS)
    partner = (seq, 1 - head)
    barrier = pltpu.get_barrier_semaphore()
    pl.semaphore_signal(barrier, inc=1, device_id=partner, device_id_type=MESH)

    def load(i):
        src, dst = (
            (k_hbm, k_own), (v_hbm, v_own), (q_hbm, q_own), (g_hbm, g_own), (lengths_hbm, lengths)
        )[i]
        return pltpu.make_async_copy(src, dst, load_sem.at[i])

    def send(src, dst, sent, landed):
        return pltpu.make_async_remote_copy(
            src_ref=src,
            dst_ref=dst,
            send_sem=send_sem.at[sent],
            recv_sem=recv_sem.at[landed],
            device_id=partner,
            device_id_type=MESH,
        )

    def far(i, g, sent=1):
        at = 2 * g + i % 2
        if i < 2:
            return send((k_own, v_own)[i].at[:, columns(g)], kv_far.at[at], sent, at)
        return send(dkv_send.at[at], dkv_far.at[at], sent, at)

    def lend(i):
        rows, wide, narrow = slice(0, HALF), slice(last * WIDE, GROUPS * WIDE), columns(last)
        src = (q_hbm.at[rows, wide], g_hbm.at[rows, wide], k_hbm.at[rows, narrow], v_hbm.at[rows, narrow])
        dst = (lent_wide if i < 2 else lent).at[i % 2]
        return send(src[i], dst, 0, 2 * GROUPS - 2 + i // 2)

    def give_back(i):
        src, dst = (given_wide, lent_wide) if i < 2 else (given, lent)
        return send(src.at[i % 2], dst.at[i % 2], 0, 2 * GROUPS - 2 + i // 2)

    def wait_lent():
        send(lent_wide, lent_wide, 0, 2 * GROUPS - 2).wait_recv()
        send(lent, lent, 0, 2 * GROUPS - 1).wait_recv()

    def wait_sent(sent, blocks):
        every = kv_far.at[0:blocks]
        send(every, every, sent, 0).wait_send()

    @pl.when(head == 0)
    def _():
        load(0).start()
        load(1).start()
        pl.semaphore_wait(barrier, 1)
        load(0).wait()
        far(0, 0, 0).start()
        load(1).wait()
        far(1, 0, 0).start()

        @pl.when(core == 1)
        def _():
            wait_sent(0, 2)

        def send_group(g, _):
            far(0, g).start()
            far(1, g).start()
            return 0

        lax.fori_loop(1, 2, send_group, 0)

        @pl.when(core == 1)
        def _():
            wait_sent(1, 2)

        lax.fori_loop(2, groups, send_group, 0)
        load(4).start()
        load(2).start()
        load(3).start()
        load(4).wait()
        bias_a[0:ROWS] = mask_bias(lengths, seq, HALF, 0, ROWS)
        bias_b[...] = mask_bias(lengths, seq, 0, 0, HALF)
        load(2).wait()
        load(3).wait()

        def local(g, _):
            for row, keys, bias in ((HALF, ROWS, bias_a), (0, HALF, bias_b)):
                kk = k_own[0:keys, columns(g)]
                vv = v_own[0:keys, columns(g)]
                qq = stacked(q_own, row, g)
                gg = stacked(g_own, row, g)
                probs = probabilities(kk, qq, bias[0:keys])
                rounded = probs.astype(BF16)
                dscores = score_gradient(probs, vv, gg)
                dv = dot_nn(rounded, gg)
                dk = dot_nn(dscores, qq)
                if row:
                    dv_sum[g] = dv
                    dk_sum[g] = dk
                else:
                    dv_sum[g, 0:HALF] += dv
                    dk_sum[g, 0:HALF] += dk
                put_heads(o_out, row, g, dot_tn(rounded, vv))
                put_heads(dq_out, row, g, dot_tn(dscores, kk) * SCALE)
            return 0

        lax.fori_loop(0, GROUPS, local, 0)

        def finish(g, _):
            far(2, g).wait_recv()
            dv_out[:, columns(g)] = (dv_sum[g] + dkv_far[2 * g].astype(F32)).astype(BF16)
            far(3, g).wait_recv()
            dk_out[:, columns(g)] = (dk_sum[g] * SCALE + dkv_far[2 * g + 1].astype(F32)).astype(BF16)
            return 0

        @pl.when(core == 1)
        def _():
            bias_lent[...] = mask_bias(lengths, seq, ROWS, 0, ROWS + HALF)
            wait_lent()
            kk = jnp.concatenate([k_own[:, columns(last)], lent[0]], axis=0)
            vv = jnp.concatenate([v_own[:, columns(last)], lent[1]], axis=0)
            qq = stacked(lent_wide.at[0], 0, 0)
            gg = stacked(lent_wide.at[1], 0, 0)
            probs = probabilities(kk, qq, bias_lent[...])
            rounded = probs.astype(BF16)
            dscores = score_gradient(probs, vv, gg)
            dv = dot_nn(rounded, gg)
            dk = dot_nn(dscores, qq) * SCALE
            dv_out[:, columns(last)] = (dv_sum[last] + dv[0:ROWS]).astype(BF16)
            dk_out[:, columns(last)] = (dk_sum[last] * SCALE + dk[0:ROWS]).astype(BF16)
            given[0] = dk[ROWS:].astype(BF16)
            given[1] = dv[ROWS:].astype(BF16)
            put_heads(given_wide.at[0], 0, 0, dot_tn(rounded, vv))
            put_heads(given_wide.at[1], 0, 0, dot_tn(dscores, kk) * SCALE)
            wait_sent(1, 2 * GROUPS - 6)
            lax.fori_loop(0, 0, finish, 0)
            for i in range(4):
                give_back(i).start()
            lax.fori_loop(0, last, finish, 0)
            wait_sent(0, 6)

        @pl.when(core == 0)
        def _():
            lax.fori_loop(0, last, finish, 0)
            wait_sent(0, 2)
            wait_sent(1, 2 * GROUPS - 2)
            finish(last, 0)

    @pl.when(head == 1)
    def _():
        pl.semaphore_wait(barrier, 1)

        @pl.when(core == 1)
        def _():
            for i in range(4):
                lend(i).start()

        for i in (4, 2, 3, 0, 1):
            load(i).start()
        load(4).wait()
        bias_a[...] = mask_bias(lengths, seq, ROWS, 0, ROWS + HALF)
        bias_b[...] = mask_bias(lengths, seq, ROWS + HALF, ROWS + HALF, HALF)
        for i in range(4):
            load(i).wait()

        def work_near(g):
            kk = k_own[HALF:ROWS, columns(g)]
            vv = v_own[HALF:ROWS, columns(g)]
            qq = stacked(q_own, HALF, g)
            gg = stacked(g_own, HALF, g)
            probs = probabilities(kk, qq, bias_b[...])
            rounded = probs.astype(BF16)
            dscores = score_gradient(probs, vv, gg)
            dv_out[HALF:ROWS, columns(g)] = dot_nn(rounded, gg).astype(BF16)
            dk_out[HALF:ROWS, columns(g)] = (dot_nn(dscores, qq) * SCALE).astype(BF16)
            put_heads(o_out, HALF, g, dot_tn(rounded, vv))
            put_heads(dq_out, HALF, g, dot_tn(dscores, kk) * SCALE)

        def work(g, _):
            work_near(g)
            k_near = k_own[0:HALF, columns(g)]
            v_near = v_own[0:HALF, columns(g)]
            qq = stacked(q_own, 0, g)
            gg = stacked(g_own, 0, g)
            near_logits = logits(k_near, qq, bias_a[ROWS:])
            near_top = jnp.max(near_logits, axis=0, keepdims=True)
            near_dprobs = dot_nt(v_near, gg)

            far(0, g).wait_recv()
            k_there = kv_far[2 * g]
            far_logits = logits(k_there, qq, bias_a[0:ROWS])
            top = jnp.maximum(near_top, jnp.max(far_logits, axis=0, keepdims=True))
            probs_far = jnp.exp2(far_logits - top)
            probs_near = jnp.exp2(near_logits - top)
            total = jnp.sum(probs_far, axis=0, keepdims=True)
            total += jnp.sum(probs_near, axis=0, keepdims=True)
            probs_far *= 1.0 / total
            probs_near *= 1.0 / total
            rounded_far = probs_far.astype(BF16)
            rounded_near = probs_near.astype(BF16)
            dkv_send[2 * g] = dot_nn(rounded_far, gg).astype(BF16)
            far(2, g).start()
            near_sum = jnp.sum(probs_near * near_dprobs, axis=0, keepdims=True)

            far(1, g).wait_recv()
            v_there = kv_far[2 * g + 1]
            dprobs = dot_nt(v_there, gg)
            delta = near_sum + jnp.sum(probs_far * dprobs, axis=0, keepdims=True)
            dscores_far = (probs_far * (dprobs - delta)).astype(BF16)
            dkv_send[2 * g + 1] = (dot_nn(dscores_far, qq) * SCALE).astype(BF16)
            far(3, g).start()
            dscores_near = (probs_near * (near_dprobs - delta)).astype(BF16)
            dv_out[0:HALF, columns(g)] = dot_nn(rounded_near, gg).astype(BF16)
            dk_out[0:HALF, columns(g)] = (dot_nn(dscores_near, qq) * SCALE).astype(BF16)
            vv = jnp.concatenate([v_there, v_near], axis=0)
            kk = jnp.concatenate([k_there, k_near], axis=0)
            rounded = jnp.concatenate([rounded_far, rounded_near], axis=0)
            dscores = jnp.concatenate([dscores_far, dscores_near], axis=0)
            put_heads(o_out, 0, g, dot_tn(rounded, vv))
            put_heads(dq_out, 0, g, dot_tn(dscores, kk) * SCALE)
            return 0

        lax.fori_loop(0, groups, work, 0)

        @pl.when(core == 1)
        def _():
            work_near(last)
            wait_sent(0, 6)
            wait_sent(1, 2 * GROUPS - 2)
            wait_lent()
            wide = slice(last * WIDE, GROUPS * WIDE)
            o_out[0:HALF, wide] = lent_wide[0]
            dq_out[0:HALF, wide] = lent_wide[1]
            dk_out[0:HALF, columns(last)] = lent[0]
            dv_out[0:HALF, columns(last)] = lent[1]

        @pl.when(core == 0)
        def _():
            wait_sent(1, 2 * GROUPS)


def store_kernel(*refs):
    count = len(refs) // 2
    copies = [
        pltpu.make_async_copy(refs[i], refs[count + i], refs[-1].at[i]) for i in range(count)
    ]
    for copy in copies:
        copy.start()
    for copy in copies:
        copy.wait()


def body(queries, keys, values, output_gradient, document_lengths):
    hbm = pl.BlockSpec(memory_space=pl.ANY)
    blocks = pltpu.VMEM((2 * GROUPS, ROWS, WIDTH), BF16)
    total = pltpu.VMEM((GROUPS, ROWS, WIDTH), F32)
    results = pl.pallas_call(
        kernel,
        out_shape=[pltpu.VMEM(x.shape, BF16) for x in (queries, queries, keys, values)],
        in_specs=[hbm] * 5,
        scratch_shapes=[
            pltpu.VMEM(queries.shape, BF16),
            pltpu.VMEM(keys.shape, BF16),
            pltpu.VMEM(values.shape, BF16),
            pltpu.VMEM(queries.shape, BF16),
            blocks, blocks, blocks, total, total,
            pltpu.VMEM((2, HALF, WIDE), BF16),
            pltpu.VMEM((2, HALF, WIDTH), BF16),
            pltpu.VMEM((2, HALF, WIDE), BF16),
            pltpu.VMEM((2, HALF, WIDTH), BF16),
            pltpu.VMEM((ROWS + HALF, HALF), F32),
            pltpu.VMEM((HALF, HALF), F32),
            pltpu.VMEM((ROWS + HALF, HALF), F32),
            pltpu.SMEM(document_lengths.shape[::-1], jnp.int32),
            pltpu.SemaphoreType.DMA((5,)),
            pltpu.SemaphoreType.DMA((2,)),
            pltpu.SemaphoreType.DMA((2 * GROUPS,)),
        ],
        compiler_params=pltpu.CompilerParams(
            collective_id=0, has_side_effects=True, vmem_limit_bytes=54 << 20
        ),
        name="packed_attention",
    )(document_lengths.T, queries, keys, values, output_gradient)
    return pl.pallas_call(
        store_kernel,
        out_shape=[jax.ShapeDtypeStruct(x.shape, BF16) for x in results],
        in_specs=[pl.BlockSpec(memory_space=pltpu.VMEM)] * len(results),
        out_specs=[hbm] * len(results),
        scratch_shapes=[pltpu.SemaphoreType.DMA((len(results),))],
        compiler_params=pltpu.CompilerParams(vmem_limit_bytes=16 << 20),
        name="store_results",
    )(*[pltpu.with_memory_space_constraint(x, pltpu.VMEM) for x in results])


def solution(mesh):
    rows = P(("seq", "head"), None)
    return jax.shard_map(
        body,
        mesh=mesh,
        in_specs=(rows, rows, rows, rows, P()),
        out_specs=(rows, rows, rows, rows),
        check_vma=False,
    )
```
